32 devices in a mesh: seq: 16 (over z, x, core), head: 2 (over y).
Axes of the slice: x: 2, y: 2, z: 4, core: 2. Of those that a mesh axis runs over, the one named last changes fastest.
Arguments:
- activations: bfloat16 [2048, 2048], P('seq'), may hold values from -6 to 6
- doc_ids: int32 [2048], replicated, may hold values from 0 to 1, as said below
- w_query: bfloat16 [2048, 2048], P(None, 'head'), may hold values from -0.125 to 0.125
- w_key: bfloat16 [2048, 2048], P(None, 'head'), may hold values from -0.125 to 0.125
- w_value: bfloat16 [2048, 2048], P(None, 'head'), may hold values from -0.125 to 0.125
- w_out: bfloat16 [2048, 2048], P('head'), may hold values from -1.5 to 1.5
- w_gate: bfloat16 [2048, 8192], P(None, 'head'), may hold values from -0.125 to 0.125
- w_up: bfloat16 [2048, 8192], P(None, 'head'), may hold values from -0.125 to 0.125
- w_down: bfloat16 [8192, 2048], P('head'), may hold values from -0.0625 to 0.0625
- gain_attn: float32 [2048], replicated, may hold values from 0.5 to 1.5
- gain_mlp: float32 [2048], replicated, may hold values from 0.5 to 1.5
- cotangent: bfloat16 [2048, 2048], P('seq'), may hold values from -6 to 6
Outputs:
- output: bfloat16 [2048, 2048], P('seq')
- input_grad: bfloat16 [2048, 2048], P('seq')
- query_grad: float32 [2048, 2048], P('seq', 'head')
- key_grad: float32 [2048, 2048], P('seq', 'head')
- value_grad: float32 [2048, 2048], P('seq', 'head')
- out_grad: float32 [2048, 2048], P('head', 'seq')
- gate_grad: float32 [2048, 8192], P('seq', 'head')
- up_grad: float32 [2048, 8192], P('seq', 'head')
- down_grad: float32 [8192, 2048], P('head', 'seq')
- gain_attn_grad: float32 [2048], P('seq')
- gain_mlp_grad: float32 [2048], P('seq')
The draws below stay inside these ranges and needn't reach their ends.
Inputs may be any that keep to these rules, and one draw needn't show every extreme that they name: `doc_ids`: document number of each token, never falling along the tokens; each document is one packed sequence of about 2048 / 2 tokens.
All inputs are finite; a program needn't handle non-finite values.
Results may differ from the reference program's by a relative error of at most 0.014.
Values may be sent and summed in bfloat16 or wider, within the bound.
No kernel may reach another device: no remote copies, remote signals or barrier semaphores. Data moves between devices by JAX's collectives and lax.ppermute only.
A program may use at most 320 MiB of HBM per device.

```python
import math
import jax
import jax.numpy as jnp
from jax import lax

D = 2048
HEADS = 16
HD = 128
FF = 8192
DOCS = 2
BIAS_LEN = 4096
TOKENS = 2048


def draw_doc_ids(key, part):
    key = jax.random.fold_in(key, 7)
    doc_len = TOKENS // DOCS
    jitter = doc_len // 4
    offsets = jax.random.randint(key, (DOCS - 1,), -jitter, jitter + 1)
    bounds = (jnp.arange(1, DOCS) * doc_len).astype(jnp.int32) + offsets.astype(jnp.int32)
    places = jnp.arange(TOKENS)
    return jnp.sum((places[:, None] >= bounds[None, :]).astype(jnp.int32), axis=1).astype(jnp.int32)


def levels(stream_key, shape, split, least, largest):
    loudness, own = 1.0, jax.random.fold_in(stream_key, 6)
    for position, shards_of in split:
        heights = jnp.exp(jax.random.uniform(jax.random.fold_in(own, position), (shards_of,), jnp.float32, least / len(split), largest / len(split)))
        loudness = loudness * jnp.repeat(heights, shape[position] // shards_of).reshape([-1 if axis == position else 1 for axis in range(len(shape))])
    return loudness


def scatter_about(rng, shape, spread, reach, split=(), kind=jnp.bfloat16):
    array = spread * jax.random.normal(rng, shape, jnp.float32)
    if split:
        array = array * levels(rng, shape, split, -0.22, 0.18)
    return jnp.clip(array, -reach, reach).astype(kind)


def setup_inputs(seed: int = 0) -> dict:
    key_list = jax.random.split(jax.random.key(seed), 13)
    return {
        "activations": scatter_about(key_list[0], (TOKENS, D), 1.0, 6.0, ((0, 16),)),
        "doc_ids": draw_doc_ids(jax.random.fold_in(key_list[12], 71), 0),
        "w_query": scatter_about(key_list[2], (D, HEADS * HD), D ** -0.5, 0.125, ((1, 2),)),
        "w_key": scatter_about(key_list[3], (D, HEADS * HD), D ** -0.5, 0.125, ((1, 2),)),
        "w_value": scatter_about(key_list[4], (D, HEADS * HD), D ** -0.5, 0.125, ((1, 2),)),
        "w_out": scatter_about(key_list[5], (HEADS * HD, D), (max(HEADS * HD // 128, 4)) ** -0.5, 1.5, ((0, 2),)),
        "w_gate": scatter_about(key_list[6], (D, FF), D ** -0.5, 0.125, ((1, 2),)),
        "w_up": scatter_about(key_list[7], (D, FF), D ** -0.5, 0.125, ((1, 2),)),
        "w_down": scatter_about(key_list[8], (FF, D), FF ** -0.5, 0.0625, ((0, 2),)),
        "gain_attn": jnp.clip(1.0 + 0.1 * jax.random.normal(key_list[9], (D,), jnp.float32), 0.5, 1.5),
        "gain_mlp": jnp.clip(1.0 + 0.1 * jax.random.normal(key_list[10], (D,), jnp.float32), 0.5, 1.5),
        "cotangent": scatter_about(key_list[11], (TOKENS, D), 1.0, 6.0, ((0, 16),)),
    }


@jax.custom_vjp
def low(v):
    return lax.optimization_barrier(v.astype(jnp.bfloat16)).astype(jnp.float32)

@jax.custom_vjp
def low_back(v):
    return v

def low_keep(v):
    return (low(v), None)

def low_pass(kept, grad):
    return (grad,)

def back_keep(v):
    return (v, None)

def back_low(kept, grad):
    return (low(grad),)
low.defvjp(low_keep, low_pass)
low_back.defvjp(back_keep, back_low)

def frequencies(head_dim):
    half_dim = head_dim // 2
    return jnp.exp(-jnp.arange(half_dim).astype(jnp.float32) * (2.0 / head_dim) * math.log(10000.0))

def turned(values, angles):
    half_dim = values.shape[-1] // 2
    cosine = jnp.cos(angles)[:, None, :]
    sine = jnp.sin(angles)[:, None, :]
    former = values[..., :half_dim]
    latter = values[..., half_dim:]
    return jnp.concatenate([former * cosine - latter * sine, former * sine + latter * cosine], axis=-1)

def normalized(values, gain):
    inverse = lax.rsqrt(lax.optimization_barrier(jnp.mean(values * values, axis=-1, keepdims=True)) + 1e-05)
    return values * inverse * gain

def forward(inputs, w_query, w_key, w_value, w_out, w_gate, w_up, w_down, gain_attn, gain_mlp, doc_ids):
    highest = lax.Precision.HIGHEST
    total = inputs.shape[0]
    places = jnp.arange(total).astype(jnp.int32)
    angles = places.astype(jnp.float32)[:, None] * frequencies(HD)[None, :]
    normed = low(normalized(inputs, gain_attn))
    query_rot = low(turned(low_back(jnp.dot(normed, w_query, precision=highest)).reshape(total, HEADS, HD), angles))
    key_rot = low(turned(low_back(jnp.dot(normed, w_key, precision=highest)).reshape(total, HEADS, HD), angles))
    value_rows = low(low_back(jnp.dot(normed, w_value, precision=highest))).reshape(total, HEADS, HD)
    block_rows = math.gcd(total, 512)
    block_starts = (jnp.arange(total // block_rows) * block_rows).astype(jnp.int32)

    def attend(first_row):
        query_block = lax.dynamic_slice_in_dim(query_rot, first_row, block_rows, 0)
        query_docs = lax.dynamic_slice_in_dim(doc_ids, first_row, block_rows, 0)
        query_places = first_row + jnp.arange(block_rows).astype(jnp.int32)
        allowed = (query_docs[:, None] == doc_ids[None, :]) & (places[None, :] <= query_places[:, None])
        scores = jnp.einsum('qhd,khd->hqk', query_block, key_rot, precision=highest) * HD ** (-0.5) - math.log(BIAS_LEN)
        scores = low_back(scores)
        attention_weights = low(jnp.where(allowed[None], jax.nn.sigmoid(scores), 0.0))
        return jnp.einsum('hqk,khd->qhd', attention_weights, value_rows, precision=highest)
    mixed = lax.map(jax.checkpoint(attend), block_starts).reshape(total, HEADS * HD)
    attended = low(low_back(mixed))
    branch = low_back(jnp.dot(attended, w_out, precision=highest))
    middle = inputs + branch
    second = low(normalized(middle, gain_mlp))
    gate = low_back(jnp.dot(second, w_gate, precision=highest))
    upward = low_back(jnp.dot(second, w_up, precision=highest))
    hidden_units = low(jax.nn.silu(gate) * upward)
    return middle + low_back(jnp.dot(hidden_units, w_down, precision=highest))

def reference(activations, doc_ids, w_query, w_key, w_value, w_out, w_gate, w_up, w_down, gain_attn, gain_mlp, cotangent):
    floats = tuple((array_item.astype(jnp.float32) for array_item in (activations, w_query, w_key, w_value, w_out, w_gate, w_up, w_down, gain_attn, gain_mlp)))

    def layer(*arrays):
        return forward(*arrays, doc_ids)
    result, pullback = jax.vjp(layer, *floats)
    grads = pullback(cotangent.astype(jnp.float32))
    return (result.astype(jnp.bfloat16), grads[0].astype(jnp.bfloat16), grads[1], grads[2], grads[3], grads[4], grads[5], grads[6], grads[7], grads[8], grads[9])
```

```python
import math

import jax
import jax.numpy as jnp
from jax import lax
from jax.sharding import PartitionSpec as P

HD = 128
BIAS_LEN = 4096
BF16 = jnp.bfloat16
F32 = jnp.float32


def frequencies(head_dim):
    half_dim = head_dim // 2
    return jnp.exp(-jnp.arange(half_dim).astype(F32) * (2.0 / head_dim) * math.log(10000.0))


def turned(values, angles):
    half_dim = values.shape[-1] // 2
    cosine = jnp.cos(angles)[:, None, :]
    sine = jnp.sin(angles)[:, None, :]
    former = values[..., :half_dim]
    latter = values[..., half_dim:]
    return jnp.concatenate(
        [former * cosine - latter * sine, former * sine + latter * cosine], axis=-1
    )


def normalized(values, gain):
    inverse = lax.rsqrt(jnp.mean(values * values, axis=-1, keepdims=True) + 1e-05)
    return values * inverse * gain, inverse


def norm_back(values, inverse, gain, upstream):
    scaled = values * inverse
    weighted = upstream * gain
    return inverse * (weighted - scaled * jnp.mean(weighted * scaled, axis=-1, keepdims=True))


def dot(one, two):
    return jnp.dot(one, two, preferred_element_type=F32)


def dot_rows(one, two):
    return lax.dot_general(one, two, (((0,), (0,)), ((), ())), preferred_element_type=F32)


def dot_back(one, two):
    return lax.dot_general(one, two, (((1,), (1,)), ((), ())), preferred_element_type=F32)


def local(
    activations,
    doc_ids,
    w_query,
    w_key,
    w_value,
    w_out,
    w_gate,
    w_up,
    w_down,
    gain_attn,
    gain_mlp,
    cotangent,
):
    rows, width = activations.shape
    devices = lax.axis_size("seq")
    total = rows * devices
    features = width // devices
    local_width = w_query.shape[1]
    heads = local_width // HD
    share = devices // (2 * heads)
    me = lax.axis_index("seq")
    core = me % 2
    residue = (me // 2) % share
    head = me // (2 * share)
    hidden = w_gate.shape[1] // 2

    def place(a, r, c):
        return (a * share + r) * 2 + c

    def split(s):
        return s // (2 * share), (s // 2) % share, s % 2

    def permuted(x, target):
        return lax.ppermute(x, "seq", [(s, target(*split(s))) for s in range(devices)])

    def core_swap(x):
        return permuted(x, lambda a, r, c: place(a, r, 1 - c))

    def pair_swap(x):
        return permuted(x, lambda a, r, c: place(a ^ 1, r, c))

    def ring_step(x):
        return permuted(x, lambda a, r, c: place((a + 2) % heads, r, c))

    def head_swap(x):
        return lax.ppermute(x, "head", [(0, 1), (1, 0)])

    head_groups = [
        [place(a, r, c) for a in range(heads)] for r in range(share) for c in range(2)
    ]
    share_groups = [
        [place(a, r, c) for r in range(share)] for a in range(heads) for c in range(2)
    ]

    def exchange(x):
        return lax.all_to_all(x, "seq", 0, 0, tiled=True, axis_index_groups=head_groups)

    def share_sum(x, dim):
        if share == 1:
            return x
        return lax.psum_scatter(
            x, "seq", scatter_dimension=dim, tiled=True, axis_index_groups=share_groups
        )

    def in_core_order(mine, other, axis):
        stacked = jnp.stack([mine, other], axis)
        return jnp.where(core == 0, stacked, jnp.flip(stacked, axis))

    def my_part(x, index, axis):
        return lax.dynamic_index_in_dim(x, index, axis, keepdims=False)

    my_places = me * rows + jnp.arange(rows, dtype=jnp.int32)
    angles = my_places.astype(F32)[:, None] * frequencies(HD)[None, :]
    block_starts = place(jnp.arange(heads, dtype=jnp.int32), residue, core) * rows
    query_places = (block_starts[:, None] + jnp.arange(rows, dtype=jnp.int32)[None, :]).reshape(-1)
    query_angles = query_places.astype(F32)[:, None] * frequencies(HD)[None, :]
    query_docs = doc_ids.reshape(heads, share, 2, rows)[:, residue, core].reshape(-1)
    allowed = (query_docs[:, None] == doc_ids[None, :]) & (
        jnp.arange(total, dtype=jnp.int32)[None, :] <= query_places[:, None]
    )
    scale = HD ** (-0.5)

    inputs = activations.astype(F32)
    normed, inverse_attn = normalized(inputs, gain_attn)
    normed_low = normed.astype(BF16)
    query = turned(dot(normed_low, w_query).reshape(rows, heads, HD), angles).astype(BF16)
    key = turned(dot(normed_low, w_key).reshape(rows, heads, HD), angles).astype(BF16)
    value = dot(normed_low, w_value).astype(BF16).reshape(rows, heads, HD)
    sent = jnp.concatenate([query, key, value], -1).transpose(1, 0, 2)
    received = exchange(sent)
    head_query = received[:, :, :HD].reshape(heads * rows, HD)
    own_kv = received[:, :, HD:]

    def all_keys(own):
        if share > 1:
            own = lax.all_gather(own, "seq", axis=1, axis_index_groups=share_groups)
        else:
            own = own[:, None]
        return in_core_order(own, core_swap(own), 2).reshape(total, 2 * HD)

    head_kv = all_keys(own_kv)
    head_key, head_value = head_kv[:, :HD], head_kv[:, HD:]
    weights = jnp.where(
        allowed, jax.nn.sigmoid(dot_back(head_query, head_key) * scale - math.log(BIAS_LEN)), 0.0
    )
    head_mixed = dot(weights.astype(BF16), head_value).astype(BF16)
    attended = exchange(head_mixed.reshape(heads, rows, HD)).transpose(1, 0, 2).reshape(rows, -1)

    def gathered(x):
        blocks = [x]
        for _ in range(heads // 2 - 1):
            blocks.append(ring_step(blocks[-1]))
        return blocks

    branch = dot(attended, w_out).astype(BF16)
    branch = branch.astype(F32) + head_swap(branch).astype(F32)
    middle = inputs + branch
    second, inverse_mlp = normalized(middle, gain_mlp)
    second_low = second.astype(BF16)

    gate_w = lax.dynamic_slice_in_dim(w_gate, core * hidden, hidden, 1)
    up_w = lax.dynamic_slice_in_dim(w_up, core * hidden, hidden, 1)
    down_w = lax.dynamic_slice_in_dim(w_down, core * hidden, hidden, 0)

    def feed_forward(normed_rows, grad_rows):
        gate = dot(normed_rows, gate_w)
        upward = dot(normed_rows, up_w)
        gate_sig = jax.nn.sigmoid(gate)
        hidden_low = (gate * gate_sig * upward).astype(BF16)
        hidden_grad = dot_back(grad_rows, down_w)
        gate_low = (hidden_grad * upward * gate_sig * (1.0 + gate * (1.0 - gate_sig))).astype(BF16)
        upward_low = (hidden_grad * gate * gate_sig).astype(BF16)
        return hidden_low, gate_low, upward_low

    chip_second = jnp.concatenate([second_low, core_swap(second_low)], 0)
    chip_cotangent = jnp.concatenate([cotangent, core_swap(cotangent)], 0)
    hidden_low, gate_low, upward_low = feed_forward(chip_second, chip_cotangent)
    second_part = dot_back(gate_low, gate_w) + dot_back(upward_low, up_w)

    def chip_sum(part):
        part = part[:rows] + core_swap(part[rows:].astype(BF16)).astype(F32)
        part = part.astype(BF16)
        return part.astype(F32) + head_swap(part).astype(F32)

    second_grad = chip_sum(second_part)
    output = (middle + chip_sum(dot(hidden_low, down_w))).astype(BF16)
    grad_out = cotangent.astype(F32)
    middle_grad = grad_out + norm_back(middle, inverse_mlp, gain_mlp, second_grad)
    branch_low = middle_grad.astype(BF16)

    mixed_grad = dot_back(branch_low, w_out).astype(BF16)
    head_mixed_grad = exchange(mixed_grad.reshape(rows, heads, HD).transpose(1, 0, 2)).reshape(
        heads * rows, HD
    )
    weights = jnp.where(
        allowed, jax.nn.sigmoid(dot_back(head_query, head_key) * scale - math.log(BIAS_LEN)), 0.0
    )
    value_part = dot_rows(weights.astype(BF16), head_mixed_grad)
    score_grad = (dot_back(head_mixed_grad, head_value) * weights * (1.0 - weights)).astype(BF16)
    query_grad = dot(score_grad, head_key) * scale
    key_part = dot_rows(score_grad, head_query) * scale
    parts = jnp.concatenate([key_part, value_part], 1).reshape(heads, share, 2, rows, 2 * HD)
    own_part = my_part(parts, core, 2) + core_swap(my_part(parts, 1 - core, 2).astype(BF16)).astype(
        F32
    )
    own_part = share_sum(own_part, 1).reshape(heads * rows, 1, 2 * HD)
    turned_back = turned(
        jnp.concatenate([query_grad[:, None], own_part[..., :HD]], 1), -query_angles
    )
    head_grads = jnp.concatenate(
        [turned_back.reshape(heads * rows, 2 * HD), own_part[:, 0, HD:]], 1
    ).astype(BF16)
    row_grads = exchange(head_grads.reshape(heads, rows, 3 * HD))
    row_grads = row_grads.reshape(heads, rows, 3, HD).transpose(2, 1, 0, 3).reshape(3, rows, -1)
    normed_part = (
        dot_back(row_grads[0], w_query)
        + dot_back(row_grads[1], w_key)
        + dot_back(row_grads[2], w_value)
    ).astype(BF16)
    normed_grad = normed_part.astype(F32) + head_swap(normed_part).astype(F32)
    input_grad = (middle_grad + norm_back(inputs, inverse_attn, gain_attn, normed_grad)).astype(BF16)

    def plane_tokens(x):
        blocks = gathered(x)
        return jnp.concatenate(blocks + [core_swap(block) for block in blocks], 0)

    plane_second = plane_tokens(second_low)
    plane_cotangent = plane_tokens(cotangent)
    plane_rows = 4 * share * features
    plane_start = (head // 2) * plane_rows
    hidden_low, gate_low, upward_low = feed_forward(plane_second, plane_cotangent)
    second_rows = lax.dynamic_slice_in_dim(plane_second, plane_start, plane_rows, 1)
    cotangent_rows = lax.dynamic_slice_in_dim(plane_cotangent, plane_start, plane_rows, 1)

    def weight_sum(partial, axis):
        shape = partial.shape
        partial = partial.reshape(shape[:axis] + (2, share * 2 * features) + shape[axis + 1 :])
        mine, other = my_part(partial, head % 2, axis), my_part(partial, 1 - head % 2, axis)
        mine = share_sum(mine + pair_swap(other.astype(BF16)).astype(F32), axis)
        mine = mine.reshape(shape[:axis] + (2, features) + shape[axis + 1 :])
        kept, given = my_part(mine, core, axis), my_part(mine, 1 - core, axis)
        both = in_core_order(kept, core_swap(given.astype(BF16)).astype(F32), 1 - axis)
        return both.reshape((features, -1) if axis == 0 else (-1, features))

    gate_sum = weight_sum(dot_rows(second_rows, gate_low), 0)
    up_sum = weight_sum(dot_rows(second_rows, upward_low), 0)
    down_sum = weight_sum(dot_rows(hidden_low, cotangent_rows), 1)

    def head_tokens(x):
        blocks = gathered(x)
        blocks = blocks + [pair_swap(block) for block in blocks]
        return blocks

    def source(index):
        ring = heads // 2
        step, paired = index % ring, index // ring
        return (head - 2 * step) % heads ^ paired

    order = jnp.stack([source(index) for index in range(heads)])

    def in_token_order(x):
        return jnp.take(x.reshape((heads, rows) + x.shape[1:]), order, axis=0).reshape(x.shape)

    def shared_sum(partial, axis):
        shape = partial.shape
        parts = partial.reshape(shape[:axis] + (heads, share, 2, features) + shape[axis + 1 :])
        mine = my_part(parts, core, axis + 2) + core_swap(
            my_part(parts, 1 - core, axis + 2).astype(BF16)
        ).astype(F32)
        return share_sum(mine, axis + 1).reshape(
            shape[:axis] + (heads, features) + shape[axis + 1 :]
        )

    all_normed = jnp.concatenate(head_tokens(normed_low), 0)
    head_sum = shared_sum(dot_rows(all_normed, in_token_order(head_grads)), 0)
    row_sum = exchange(head_sum.astype(BF16)).astype(F32)
    row_sum = row_sum.reshape(heads, features, 3, HD).transpose(2, 1, 0, 3).reshape(3, features, -1)

    all_attended = jnp.concatenate(head_tokens(attended), 0)
    chip_columns = width // heads
    sent_branch = exchange(branch_low.reshape(rows, heads, chip_columns).transpose(1, 0, 2))
    out_part = dot_rows(all_attended, in_token_order(sent_branch.reshape(heads * rows, -1)))
    out_part = out_part.reshape(local_width, share, 2, features)
    out_sum = my_part(out_part, core, 2) + core_swap(
        my_part(out_part, 1 - core, 2).astype(BF16)
    ).astype(F32)
    out_sum = share_sum(out_sum, 1).reshape(local_width, features)

    my_start = me * features

    def gain_sum(pairs, gain):
        term = 0.0
        for weight, grad in pairs:
            own = lax.dynamic_slice_in_dim(weight, my_start, features, 0).astype(F32)
            term = term + jnp.sum(own * grad, axis=1)
        return term / lax.dynamic_slice_in_dim(gain, my_start, features, 0)

    gains = jnp.stack(
        [
            gain_sum(((w_query, row_sum[0]), (w_key, row_sum[1]), (w_value, row_sum[2])), gain_attn),
            gain_sum(((w_gate, gate_sum), (w_up, up_sum)), gain_mlp),
        ]
    )
    gains = gains + head_swap(gains)
    return (
        output,
        input_grad,
        row_sum[0],
        row_sum[1],
        row_sum[2],
        out_sum,
        gate_sum,
        up_sum,
        down_sum,
        gains[0],
        gains[1],
    )


def solution(mesh):
    placed = (
        P("seq", None),
        P(),
        P(None, "head"),
        P(None, "head"),
        P(None, "head"),
        P("head", None),
        P(None, "head"),
        P(None, "head"),
        P("head", None),
        P(),
        P(),
        P("seq", None),
    )
    return jax.shard_map(
        local,
        mesh=mesh,
        in_specs=placed,
        out_specs=(
            P("seq", None),
            P("seq", None),
            P("seq", "head"),
            P("seq", "head"),
            P("seq", "head"),
            P("head", "seq"),
            P("seq", "head"),
            P("seq", "head"),
            P("head", "seq"),
            P("seq"),
            P("seq"),
        ),
        check_vma=False,
    )
```

```python
import functools
import math

import jax
import jax.numpy as jnp
from jax import lax
from jax.experimental import pallas as pl
from jax.experimental.pallas import tpu as pltpu
from jax.sharding import PartitionSpec as P

HD = 128
BIAS_LEN = 4096
BF16 = jnp.bfloat16
F32 = jnp.float32
TILE = 256
KEYS = 1024
VMEM = 60 * 1024 * 1024


def frequencies(head_dim):
    half_dim = head_dim // 2
    return jnp.exp(-jnp.arange(half_dim).astype(F32) * (2.0 / head_dim) * math.log(10000.0))


def turning(places, sign):
    angles = places.astype(F32)[..., None] * frequencies(HD)
    cosine, sine = jnp.cos(angles), sign * jnp.sin(angles)
    return jnp.concatenate([cosine, cosine], -1), jnp.concatenate([-sine, sine], -1)


def normalized(values, gain):
    inverse = lax.rsqrt(jnp.mean(values * values, axis=-1, keepdims=True) + 1e-05)
    return values * inverse * gain, inverse


def norm_back(values, inverse, gain, upstream):
    scaled = values * inverse
    weighted = upstream * gain
    return inverse * (weighted - scaled * jnp.mean(weighted * scaled, axis=-1, keepdims=True))


def dot(one, two):
    return jnp.dot(one, two, preferred_element_type=F32)


def dot_rows(one, two):
    return lax.dot_general(one, two, (((0,), (0,)), ((), ())), preferred_element_type=F32)


def dot_back(one, two):
    return lax.dot_general(one, two, (((1,), (1,)), ((), ())), preferred_element_type=F32)


def gated(normed, hidden_grad, gate_w, up_w):
    gate = dot(normed, gate_w)
    upward = dot(normed, up_w)
    gate_sig = jax.nn.sigmoid(gate)
    silu = gate * gate_sig
    hidden_low = (silu * upward).astype(BF16)
    gate_low = (hidden_grad * upward * (gate_sig + silu * (1.0 - gate_sig))).astype(BF16)
    upward_low = (hidden_grad * silu).astype(BF16)
    return hidden_low, gate_low, upward_low


def call(kernel, scalars, grid, in_specs, out_specs, shapes, scratch, flops=0, moved=0, exps=0):
    return pl.pallas_call(
        kernel,
        grid_spec=pltpu.PrefetchScalarGridSpec(
            num_scalar_prefetch=1,
            grid=grid,
            in_specs=in_specs,
            out_specs=out_specs,
            scratch_shapes=scratch,
        ),
        out_shape=shapes,
        compiler_params=pltpu.CompilerParams(vmem_limit_bytes=VMEM),
        cost_estimate=pl.CostEstimate(flops=flops, bytes_accessed=moved, transcendentals=exps),
    )


def array(shape, kind):
    return jax.ShapeDtypeStruct(tuple(shape), kind)


def whole(shape, **more):
    return pl.BlockSpec(tuple(shape), lambda step, place: (0,) * len(shape), **more)


def half_turn(values, cosine, sine):
    return values * cosine + pltpu.roll(values, HD // 2, 1) * sine


def heads_kernel(heads, place, x, gain, cosine, sine, w_query, w_key, w_value, normed, *refs):
    blocks, held = refs[:heads], refs[heads]
    step = pl.program_id(0)

    @pl.when(step == 0)
    def _():
        values = x[...].astype(F32)
        inverse = lax.rsqrt(jnp.mean(values * values, axis=-1, keepdims=True) + 1e-05)
        normed[...] = (values * inverse * gain[...]).astype(BF16)

    low = normed[...]
    count = w_query.shape[1] // HD
    for index, weight in enumerate((w_query, w_key, w_value)):
        part = dot(low, weight[...])
        for head in range(count):
            values = part[:, head * HD : (head + 1) * HD]
            if index < 2:
                values = half_turn(values, cosine[...], sine[...])
            held[step * count + head, :, index * HD : (index + 1) * HD] = values.astype(BF16)

    @pl.when(step == pl.num_programs(0) - 1)
    def _():
        for index, block in enumerate(blocks):
            block[...] = held[place[0] ^ index]


def head_blocks(head, x, gain, cosine, sine, w_query, w_key, w_value):
    rows, width = x.shape
    heads = w_query.shape[1] // HD
    weight = pl.BlockSpec((width, 2 * HD), lambda step, place: (0, step))
    block = (rows, 3 * HD)
    out = call(
        functools.partial(heads_kernel, heads),
        head,
        (heads // 2,),
        [whole((rows, width)), whole((1, width)), whole((rows, HD)), whole((rows, HD))]
        + [weight] * 3,
        [whole((rows, width))] + [whole(block)] * heads,
        [array((rows, width), BF16)] + [array(block, BF16)] * heads,
        [pltpu.VMEM((heads,) + block, BF16)],
        flops=6 * rows * width * heads * HD,
        moved=6 * width * heads * HD,
    )(head, x, gain[None], cosine, sine, w_query, w_key, w_value)
    return out[0], out[1:]


def join_kernel(heads, place, *refs):
    query, pair = refs[heads:]
    for index, block in enumerate(refs[:heads]):
        query[place[0] ^ index] = block[:, :HD]
        pair[place[0] ^ index] = block[:, HD:]


def joined(head, blocks):
    heads, (rows, width) = len(blocks), blocks[0].shape
    return call(
        functools.partial(join_kernel, heads),
        head,
        (1,),
        [whole((rows, width))] * heads,
        [whole((heads, rows, HD)), whole((heads, rows, 2 * HD))],
        [array((heads, rows, HD), BF16), array((heads, rows, 2 * HD), BF16)],
        [],
        moved=4 * heads * rows * width,
    )(head, *blocks)


def out_back_kernel(
    heads, place, middle, mine, theirs, gain, cotangent, weight, middle_grad, *refs
):
    blocks, (low, held) = refs[:heads], refs[heads:]
    step = pl.program_id(0)

    @pl.when(step == 0)
    def _():
        values = middle[...]
        inverse = lax.rsqrt(jnp.mean(values * values, axis=-1, keepdims=True) + 1e-05)
        upstream = mine[...].astype(F32) + theirs[...].astype(F32)
        grad = cotangent[...].astype(F32) + norm_back(values, inverse, gain[...], upstream)
        middle_grad[...] = grad
        low[...] = grad.astype(BF16)

    part = dot_back(low[...], weight[...]).astype(BF16)
    for index in range(2):
        held[2 * step + index, :, :HD] = part[:, index * HD : (index + 1) * HD]

    @pl.when(step == pl.num_programs(0) - 1)
    def _():
        columns = low.shape[1] // heads
        for head in range(heads):
            held[head, :, HD:] = low[:, head * columns : (head + 1) * columns]
        for index, block in enumerate(blocks):
            block[...] = held[place[0] ^ index]


def out_back(head, middle, mine, theirs, gain, cotangent, w_out):
    rows, width = middle.shape
    heads = w_out.shape[0] // HD
    block = (rows, HD + width // heads)
    full = whole((rows, width))
    out = call(
        functools.partial(out_back_kernel, heads),
        head,
        (heads // 2,),
        [full, full, full, whole((1, width)), full]
        + [pl.BlockSpec((2 * HD, width), lambda step, place: (step, 0))],
        [full] + [whole(block)] * heads,
        [array((rows, width), F32)] + [array(block, BF16)] * heads,
        [pltpu.VMEM((rows, width), BF16), pltpu.VMEM((heads,) + block, BF16)],
        flops=2 * rows * width * heads * HD,
        moved=2 * width * heads * HD,
    )(head, middle, mine, theirs, gain[None], cotangent, w_out)
    return out[0], out[1:]


def back_kernel(
    share, ring, place, query, pair, starts, places, cosine, sine, *refs
):
    heads, rows = query.shape[:2]
    blocks, (query_grad, own, other, columns, upstream, held, total) = refs[:heads], refs[heads:]
    for index, block in enumerate(blocks):
        upstream[place[3] ^ index] = block[:, :HD]
        held[place[3] ^ index] = block[:, HD:]
    for index, source in enumerate(ring):
        columns[index] = held[source]
    core = place[2]
    group = 2 * share * rows
    scale = HD ** (-0.5)
    total[...] = jnp.zeros_like(total)
    for block in range(heads):
        q, grad = query[block], upstream[block]
        start, spot = starts[block : block + 1], places[block : block + 1]
        sum_query = jnp.zeros((rows, HD), F32)
        for first in range(0, (block + 1) * group, KEYS):
            size = min(KEYS, (block + 1) * group - first)
            keys = pl.ds(first, size)
            k, v = pair[keys, :HD], pair[keys, HD:]
            scores = dot_back(k, q) * scale - math.log(BIAS_LEN)
            key_places = first + lax.broadcasted_iota(jnp.int32, (size, rows), 0)
            allowed = (key_places >= start) & (key_places <= spot)
            weights = jnp.where(allowed, jax.nn.sigmoid(scores), 0.0)
            total[keys, HD:] += dot(weights.astype(BF16), grad)
            score_grad = (dot_back(v, grad) * weights * (1.0 - weights)).astype(BF16)
            total[keys, :HD] += dot(score_grad, q) * scale
            sum_query += dot_rows(score_grad, k)
        query_grad[block] = half_turn(sum_query * scale, cosine[block], sine[block]).astype(BF16)
    both = total[...].reshape(heads * share, 2, rows, 2 * HD)
    mine, theirs = both[:, 0], both[:, 1]
    own[...] = jnp.where(core == 0, mine, theirs)
    other[...] = jnp.where(core == 0, theirs, mine).astype(BF16)


def attention_back(place, share, ring, query, pair, blocks, starts, places, cosine, sine):
    heads, rows = query.shape[:2]
    total = pair.shape[0]
    halves = (heads * share, rows, 2 * HD)
    block = (heads, rows, HD)
    columns = (heads, rows, blocks[0].shape[1] - HD)
    return call(
        functools.partial(back_kernel, share, ring),
        place,
        (1,),
        [whole(block), whole(pair.shape), whole((heads, rows)), whole((heads, rows))]
        + [whole(block)] * 2
        + [whole(blocks[0].shape)] * heads,
        [whole(block), whole(halves), whole(halves), whole(columns)],
        [array(block, BF16), array(halves, F32), array(halves, BF16), array(columns, BF16)],
        [pltpu.VMEM(block, BF16), pltpu.VMEM(columns, BF16), pltpu.VMEM((total, 2 * HD), F32)],
        flops=10 * heads * rows * total * HD // 2,
        moved=8 * total * HD,
        exps=heads * rows * total,
    )(place, query, pair, starts, places, cosine, sine, *blocks)


def grads_kernel(ring, place, query_grad, own, received, cosine, sine, ordered, *refs):
    heads = len(ring)
    blocks, held = refs[:heads], refs[heads]
    for index in range(heads):
        both = own[index] + received[index].astype(F32)
        key = half_turn(both[:, :HD], cosine[index], sine[index])
        held[index, :, :HD] = query_grad[index]
        held[index, :, HD : 2 * HD] = key.astype(BF16)
        held[index, :, 2 * HD :] = both[:, HD:].astype(BF16)
    for index, source in enumerate(ring):
        ordered[index] = held[source]
        blocks[index][...] = held[place[0] ^ index]


def grad_blocks(head, ring, query_grad, own, received, cosine, sine):
    heads, rows = query_grad.shape[:2]
    block = (heads, rows, HD)
    out = call(
        functools.partial(grads_kernel, ring),
        head,
        (1,),
        [whole(block), whole(own.shape), whole(received.shape), whole(block), whole(block)],
        [whole((heads, rows, 3 * HD))] + [whole((rows, 3 * HD))] * heads,
        [array((heads, rows, 3 * HD), BF16)] + [array((rows, 3 * HD), BF16)] * heads,
        [pltpu.VMEM((heads, rows, 3 * HD), BF16)],
        moved=20 * heads * rows * HD,
    )(head, query_grad, own, received, cosine, sine)
    return out[0], out[1:]


def project_back_kernel(heads, place, *refs):
    blocks, (w_query, w_key, w_value, out, held) = refs[:heads], refs[heads:]

    @pl.when(pl.program_id(0) == 0)
    def _():
        for index, block in enumerate(blocks):
            columns = pl.ds(pl.multiple_of((place[0] ^ index) * HD, HD), HD)
            for part in range(3):
                held[part, :, columns] = block[:, part * HD : (part + 1) * HD]

    out[...] = (
        dot_back(held[0], w_query[...])
        + dot_back(held[1], w_key[...])
        + dot_back(held[2], w_value[...])
    ).astype(BF16)


def projected_back(head, blocks, w_query, w_key, w_value):
    heads, (rows, columns) = len(blocks), blocks[0].shape
    width, local_width = w_query.shape
    weight = pl.BlockSpec((2 * TILE, local_width), lambda step, place: (step, 0))
    return call(
        functools.partial(project_back_kernel, heads),
        head,
        (width // (2 * TILE),),
        [whole((rows, columns))] * heads + [weight] * 3,
        pl.BlockSpec((rows, 2 * TILE), lambda step, place: (0, step)),
        array((rows, width), BF16),
        [pltpu.VMEM((3, rows, local_width), BF16)],
        flops=6 * rows * width * local_width,
        moved=6 * width * local_width,
    )(head, *blocks, w_query, w_key, w_value)


def chip_kernel(
    half, own_normed, other_normed, hidden_grad, gate_w, up_w,
    back_own, back_other, hidden, normed, back_sum,
):
    step = pl.program_id(0)
    rows = own_normed.shape[0]

    @pl.when(step == 0)
    def _():
        normed[:rows] = own_normed[...]
        normed[rows:] = other_normed[...]
        back_sum[...] = jnp.zeros_like(back_sum)

    hidden[...], gate_low, upward_low = gated(
        normed[...], hidden_grad[...].astype(F32), gate_w[...], up_w[...]
    )
    back_sum[...] += dot_back(gate_low, gate_w[...]) + dot_back(upward_low, up_w[...])

    @pl.when(step == pl.num_programs(0) - 1)
    def _():
        back_own[...] = back_sum[:rows]
        back_other[...] = back_sum[rows:].astype(BF16)


def feed_kernel(half, hidden, weight, feed_own, feed_other, total):
    step = pl.program_id(0)

    @pl.when(step == 0)
    def _():
        total[...] = jnp.zeros_like(total)

    total[...] += dot(hidden[...], weight[...])

    @pl.when(step == pl.num_programs(0) - 1)
    def _():
        rows = feed_own.shape[0]
        feed_own[...] = total[:rows]
        feed_other[...] = total[rows:].astype(BF16)


def weight_specs(width, first, steps):
    def tile(step, place):
        return place[0] * steps + first + step

    columns = pl.BlockSpec((width, TILE), lambda step, place: (0, tile(step, place)))
    return [columns, columns, pl.BlockSpec((TILE, width), lambda step, place: (tile(step, place), 0))]


def chip_back(half, own_normed, other_normed, hidden_grad, weights):
    rows, width = own_normed.shape
    steps = weights[0].shape[1] // 2 // TILE
    block = whole((rows, width))
    tile = pl.BlockSpec((2 * rows, TILE), lambda step, place: (0, step))
    return call(
        chip_kernel,
        half,
        (steps,),
        [block] * 2 + [tile] + weight_specs(width, 0, steps)[:2],
        [block] * 2 + [tile],
        [
            array((rows, width), F32),
            array((rows, width), BF16),
            array((2 * rows, steps * TILE), BF16),
        ],
        [pltpu.VMEM((2 * rows, width), BF16), pltpu.VMEM((2 * rows, width), F32)],
        flops=16 * rows * width * steps * TILE,
        moved=4 * width * steps * TILE,
        exps=2 * rows * steps * TILE,
    )(half, own_normed, other_normed, hidden_grad, *weights[:2])


def chip_feed(half, hidden, w_down):
    tokens, units = hidden.shape
    width = w_down.shape[1]
    steps = units // (2 * TILE)
    block = whole((tokens // 2, width))
    return call(
        feed_kernel,
        half,
        (steps,),
        [
            pl.BlockSpec((tokens, 2 * TILE), lambda step, place: (0, step)),
            pl.BlockSpec((2 * TILE, width), lambda step, place: (place[0] * steps + step, 0)),
        ],
        [block] * 2,
        [array((tokens // 2, width), F32), array((tokens // 2, width), BF16)],
        [pltpu.VMEM((tokens, width), F32)],
        flops=2 * tokens * width * units,
        moved=2 * width * units,
    )(half, hidden, w_down)


def hidden_grad_kernel(place, grads, weight, out):
    for first in range(0, grads.shape[0], TILE):
        rows = pl.ds(first, TILE)
        out[rows] = dot_back(grads[rows], weight[...]).astype(BF16)


def hidden_grads(place, grads, w_down):
    tokens, width = grads.shape
    steps = w_down.shape[0] // 2 // (2 * TILE)
    return call(
        hidden_grad_kernel,
        place,
        (steps,),
        [
            whole((tokens, width), pipeline_mode=pl.Buffered(1)),
            pl.BlockSpec((2 * TILE, width), lambda step, place: (place[0] * steps + step, 0)),
        ],
        pl.BlockSpec((tokens, 2 * TILE), lambda step, place: (0, step)),
        array((tokens, steps * 2 * TILE), BF16),
        [],
        flops=4 * tokens * width * steps * TILE,
        moved=4 * width * steps * TILE,
    )(place, grads, w_down)


def plane_kernel(
    share, place, normed, normed_columns, grad_columns, hidden_grad, gate_w, up_w,
    kept, given, normed_turned, grad_turned, hidden, gate, upward,
):
    @pl.when(pl.program_id(0) == 0)
    def _():
        normed_turned[...] = normed_columns[...].T
        grad_turned[...] = grad_columns[...].T

    for first in range(0, normed.shape[0], TILE):
        rows = pl.ds(first, TILE)
        hidden[rows], gate[rows], upward[rows] = gated(
            normed[rows], hidden_grad[rows].astype(F32), gate_w[...], up_w[...]
        )
    core = place[2]
    for index, (left, right) in enumerate(
        ((normed_turned, gate), (normed_turned, upward), (grad_turned, hidden))
    ):
        both = dot(left[...], right[...]).reshape(2 * share, 2, -1, TILE)
        mine, theirs = both[:, 0].reshape(-1, TILE), both[:, 1].reshape(-1, TILE)
        kept[index] = jnp.where(core == 0, mine, theirs)
        given[index] = jnp.where(core == 0, theirs, mine).astype(BF16)


def plane_weight_grads(place, share, normed, grads, hidden_grad, weights, first, tiles):
    tokens, width = normed.shape
    steps = weights[0].shape[1] // 2 // TILE
    columns = width // 4
    out = pl.BlockSpec((3, columns // 2, TILE), lambda step, place: (0, 0, step))
    held = pl.BlockSpec((tokens, columns), lambda step, place: (0, place[1]))
    return call(
        functools.partial(plane_kernel, share),
        place,
        (tiles,),
        [
            whole((tokens, width), pipeline_mode=pl.Buffered(1)),
            held,
            held,
            pl.BlockSpec((tokens, TILE), lambda step, place: (0, first + step)),
        ]
        + weight_specs(width, first, steps)[:2],
        [out, out],
        [array((3, columns // 2, tiles * TILE), kind) for kind in (F32, BF16)],
        [pltpu.VMEM((columns, tokens), BF16)] * 2 + [pltpu.VMEM((tokens, TILE), BF16)] * 3,
        flops=2 * tokens * (2 * width + 3 * columns) * tiles * TILE,
        moved=4 * width * tiles * TILE,
        exps=tokens * tiles * TILE,
    )(place, normed, normed, grads, hidden_grad, *weights[:2])


def local(
    activations,
    doc_ids,
    w_query,
    w_key,
    w_value,
    w_out,
    w_gate,
    w_up,
    w_down,
    gain_attn,
    gain_mlp,
    cotangent,
):
    rows, width = activations.shape
    devices = lax.axis_size("seq")
    total = rows * devices
    features = width // devices
    local_width = w_query.shape[1]
    heads = local_width // HD
    share = devices // (2 * heads)
    me = lax.axis_index("seq")
    core = me % 2
    residue = (me // 2) % share
    head = me // (2 * share)
    tiles = w_gate.shape[1] // 2 // TILE
    feed_weights = (w_gate, w_up, w_down)

    def place(a, r, c):
        return (a * share + r) * 2 + c

    def split(s):
        return s // (2 * share), (s // 2) % share, s % 2

    def permuted(x, target):
        return lax.ppermute(x, "seq", [(s, target(*split(s))) for s in range(devices)])

    def core_swap(x):
        return permuted(x, lambda a, r, c: place(a, r, 1 - c))

    def pair_swap(x):
        return permuted(x, lambda a, r, c: place(a ^ 1, r, c))

    ring = [*range(0, heads, 2), *range(heads - 1, 0, -2)]
    ring_groups = [[place(a, r, c) for a in ring] for r in range(share) for c in range(2)]

    def gathered(x):
        return lax.all_gather(x, "seq", axis=0, tiled=True, axis_index_groups=ring_groups)

    def head_swap(x):
        return lax.ppermute(x, "head", [(0, 1), (1, 0)])

    head_groups = [
        [place(a, r, c) for a in range(heads)] for r in range(share) for c in range(2)
    ]
    share_groups = [
        [place(a, r, c) for r in range(share)] for a in range(heads) for c in range(2)
    ]

    def spread(blocks):
        sent = [permuted(block, lambda a, r, c, i=i: place(a ^ i, r, c)) for i, block in enumerate(blocks) if i]
        return [blocks[0], *sent]

    def after(x, *earlier):
        return lax.optimization_barrier((x, *earlier))[0]

    def exchange(x):
        return lax.all_to_all(x, "seq", 0, 0, tiled=True, axis_index_groups=head_groups)

    def share_sum(x, dim):
        if share == 1:
            return x
        return lax.psum_scatter(
            x, "seq", scatter_dimension=dim, tiled=True, axis_index_groups=share_groups
        )

    def in_core_order(mine, other, axis):
        return jnp.where(core == 0, jnp.stack([mine, other], axis), jnp.stack([other, mine], axis))

    def my_part(x, index, axis):
        return lax.dynamic_index_in_dim(x, index, axis, keepdims=False)

    my_places = me * rows + jnp.arange(rows, dtype=jnp.int32)
    block_starts = place(jnp.arange(heads, dtype=jnp.int32), residue, core) * rows
    query_places = block_starts[:, None] + jnp.arange(rows, dtype=jnp.int32)[None, :]
    query_docs = doc_ids.reshape(heads, share, 2, rows)[:, residue, core]
    query_starts = jnp.sum((doc_ids < query_docs[..., None]).astype(jnp.int32), -1)
    key_places = jnp.arange(total, dtype=jnp.int32)
    allowed = (key_places >= query_starts.reshape(-1, 1)) & (
        key_places <= query_places.reshape(-1, 1)
    )
    scale = HD ** (-0.5)
    head_index = head[None].astype(jnp.int32)
    position = jnp.stack([head % 2, head // 2, core, head]).astype(jnp.int32)

    plane_cotangent = gathered(cotangent)
    inputs = activations.astype(F32)
    cosine, sine = turning(my_places, 1.0)
    normed_low, blocks = head_blocks(
        head_index, activations, gain_attn, cosine, sine, w_query, w_key, w_value
    )
    head_query, own_kv = joined(head_index, spread(blocks))
    core_index = core[None].astype(jnp.int32)
    chip_cotangent = jnp.concatenate([cotangent, core_swap(cotangent)], 0)
    chip_hidden_grad = hidden_grads(core_index, after(chip_cotangent, *blocks), w_down)

    def all_keys(own):
        if share > 1:
            own = lax.all_gather(own, "seq", axis=1, axis_index_groups=share_groups)
        else:
            own = own[:, None]
        return in_core_order(own, core_swap(own), 2).reshape(total, 2 * HD)

    head_kv = all_keys(own_kv)
    scores = dot_back(head_query.reshape(heads * rows, HD), head_kv[:, :HD])
    weights = jnp.where(allowed, jax.nn.sigmoid(scores * scale - math.log(BIAS_LEN)), 0.0)
    head_mixed = dot(weights.astype(BF16), head_kv[:, HD:]).astype(BF16)
    attended = exchange(head_mixed.reshape(heads, rows, HD)).transpose(1, 0, 2).reshape(rows, -1)

    branch = dot(attended, w_out).astype(BF16)
    branch = branch.astype(F32) + head_swap(branch).astype(F32)
    middle = inputs + branch
    second, inverse_mlp = normalized(middle, gain_mlp)
    second_low = second.astype(BF16)

    back_own, back_other, hidden = chip_back(
        core_index, second_low, core_swap(second_low), chip_hidden_grad, feed_weights
    )

    def core_sum(own, other):
        return (own + core_swap(other).astype(F32)).astype(BF16)

    back_low = core_sum(back_own, back_other)
    back_received = head_swap(back_low)
    feed_low = core_sum(*chip_feed(core_index, after(hidden, back_low), w_down))
    middle_grad, blocks = out_back(
        head_index, middle, back_low, back_received, gain_mlp, cotangent, w_out
    )
    feed_received = head_swap(after(feed_low, blocks[0]))
    output = (middle + (feed_low.astype(F32) + feed_received.astype(F32))).astype(BF16)
    plane_second = gathered(second_low)
    all_normed = gathered(after(normed_low, blocks[0]))
    all_attended = gathered(after(attended, blocks[0]))
    hidden_grad = hidden_grads(position, after(plane_cotangent, chip_hidden_grad), w_down)

    def plane_piece(first, count):
        kept, given = plane_weight_grads(
            position, share, plane_second, plane_cotangent, hidden_grad, feed_weights, first, count
        )
        kept = kept + core_swap(given).astype(F32)
        kept = share_sum(kept.reshape(6, share, features, -1), 1).reshape(3, 2, features, -1)
        mine, other = my_part(kept, head % 2, 1), my_part(kept, 1 - head % 2, 1)
        return mine, pair_swap(other.astype(BF16)).astype(F32), given

    received = spread(blocks)
    pieces = [plane_piece(0, tiles // 2)]
    received = [after(block, pieces[0][2]) for block in received]
    cosines, sines = turning(query_places, -1.0)
    query_grad, own_grad, other_grad, sent_branch = attention_back(
        position,
        share,
        tuple(ring),
        head_query,
        head_kv,
        received,
        query_starts,
        query_places,
        cosines,
        sines,
    )
    own_grad, received = own_grad, core_swap(other_grad)
    if share > 1:
        shape = (heads, share, rows, 2 * HD)
        own_grad = share_sum((own_grad + received.astype(F32)).reshape(shape), 1)[:, 0]
        received = jnp.zeros(own_grad.shape, BF16)
    ring_grads, blocks = grad_blocks(
        head_index, tuple(ring), query_grad, own_grad, received, cosines, sines
    )
    received = spread(blocks)
    pieces.append(plane_piece(tiles // 2, tiles // 2))
    received = [after(block, pieces[1][2]) for block in received]
    normed_part = projected_back(head_index, received, w_query, w_key, w_value)
    normed_grad = normed_part.astype(F32) + head_swap(normed_part).astype(F32)
    inverse_attn = lax.rsqrt(jnp.mean(inputs * inputs, axis=-1, keepdims=True) + 1e-05)
    input_grad = (middle_grad + norm_back(inputs, inverse_attn, gain_attn, normed_grad)).astype(BF16)

    mine = jnp.concatenate([piece[0] for piece in pieces], -1)
    other = jnp.concatenate([piece[1] for piece in pieces], -1)
    feed_sums = jnp.where(
        head % 2 == 0, jnp.concatenate([mine, other], -1), jnp.concatenate([other, mine], -1)
    )
    gate_sum, up_sum, down_sum = feed_sums[0], feed_sums[1], feed_sums[2].T

    def shared_sum(partial, axis):
        shape = partial.shape
        parts = partial.reshape(shape[:axis] + (heads, share, 2, features) + shape[axis + 1 :])
        mine = my_part(parts, core, axis + 2) + core_swap(
            my_part(parts, 1 - core, axis + 2).astype(BF16)
        ).astype(F32)
        return share_sum(mine, axis + 1).reshape(
            shape[:axis] + (heads, features) + shape[axis + 1 :]
        )

    head_sum = shared_sum(dot_rows(all_normed, ring_grads.reshape(heads * rows, -1)), 0)
    row_sum = exchange(head_sum.astype(BF16)).astype(F32)
    row_sum = row_sum.reshape(heads, features, 3, HD).transpose(2, 1, 0, 3).reshape(3, features, -1)

    out_part = dot_rows(all_attended, sent_branch.reshape(heads * rows, -1))
    out_part = out_part.reshape(local_width, share, 2, features)
    out_sum = my_part(out_part, core, 2) + core_swap(
        my_part(out_part, 1 - core, 2).astype(BF16)
    ).astype(F32)
    out_sum = share_sum(out_sum, 1).reshape(local_width, features)

    my_start = me * features

    def gain_sum(pairs, gain):
        term = 0.0
        for weight, grad in pairs:
            own = lax.dynamic_slice_in_dim(weight, my_start, features, 0).astype(F32)
            term = term + jnp.sum(own * grad, axis=1)
        return term / lax.dynamic_slice_in_dim(gain, my_start, features, 0)

    gains = jnp.stack(
        [
            gain_sum(((w_query, row_sum[0]), (w_key, row_sum[1]), (w_value, row_sum[2])), gain_attn),
            gain_sum(((w_gate, gate_sum), (w_up, up_sum)), gain_mlp),
        ]
    )
    gains = gains + head_swap(gains)
    return (
        output,
        input_grad,
        row_sum[0],
        row_sum[1],
        row_sum[2],
        out_sum,
        gate_sum,
        up_sum,
        down_sum,
        gains[0],
        gains[1],
    )


def solution(mesh):
    placed = (
        P("seq", None),
        P(),
        P(None, "head"),
        P(None, "head"),
        P(None, "head"),
        P("head", None),
        P(None, "head"),
        P(None, "head"),
        P("head", None),
        P(),
        P(),
        P("seq", None),
    )
    return jax.shard_map(
        local,
        mesh=mesh,
        in_specs=placed,
        out_specs=(
            P("seq", None),
            P("seq", None),
            P("seq", "head"),
            P("seq", "head"),
            P("seq", "head"),
            P("head", "seq"),
            P("seq", "head"),
            P("seq", "head"),
            P("head", "seq"),
            P("seq"),
            P("seq"),
        ),
        check_vma=False,
    )
```

```python
import functools
import math

import jax
import jax.numpy as jnp
from jax import lax
from jax.experimental import pallas as pl
from jax.experimental.pallas import tpu as pltpu
from jax.sharding import PartitionSpec as P

HD = 128
BIAS_LEN = 4096
BF16 = jnp.bfloat16
F32 = jnp.float32
TILE = 256
KEYS = 1024
VMEM = 60 * 1024 * 1024


def frequencies(head_dim):
    half_dim = head_dim // 2
    return jnp.exp(-jnp.arange(half_dim).astype(F32) * (2.0 / head_dim) * math.log(10000.0))


def turning(places, sign):
    angles = places.astype(F32)[..., None] * frequencies(HD)
    cosine, sine = jnp.cos(angles), sign * jnp.sin(angles)
    return jnp.concatenate([cosine, cosine], -1), jnp.concatenate([-sine, sine], -1)


def normalized(values, gain):
    inverse = lax.rsqrt(jnp.mean(values * values, axis=-1, keepdims=True) + 1e-05)
    return values * inverse * gain, inverse


def norm_back(values, inverse, gain, upstream):
    scaled = values * inverse
    weighted = upstream * gain
    return inverse * (weighted - scaled * jnp.mean(weighted * scaled, axis=-1, keepdims=True))


def dot(one, two):
    return jnp.dot(one, two, preferred_element_type=F32)


def dot_rows(one, two):
    return lax.dot_general(one, two, (((0,), (0,)), ((), ())), preferred_element_type=F32)


def dot_back(one, two):
    return lax.dot_general(one, two, (((1,), (1,)), ((), ())), preferred_element_type=F32)


def gated(normed, hidden_grad, gate_w, up_w):
    gate = dot(normed, gate_w)
    upward = dot(normed, up_w)
    gate_sig = jax.nn.sigmoid(gate)
    silu = gate * gate_sig
    hidden_low = (silu * upward).astype(BF16)
    gate_low = (hidden_grad * upward * (gate_sig + silu * (1.0 - gate_sig))).astype(BF16)
    upward_low = (hidden_grad * silu).astype(BF16)
    return hidden_low, gate_low, upward_low


def call(kernel, scalars, grid, in_specs, out_specs, shapes, scratch, flops=0, moved=0, exps=0):
    return pl.pallas_call(
        kernel,
        grid_spec=pltpu.PrefetchScalarGridSpec(
            num_scalar_prefetch=1,
            grid=grid,
            in_specs=in_specs,
            out_specs=out_specs,
            scratch_shapes=scratch,
        ),
        out_shape=shapes,
        compiler_params=pltpu.CompilerParams(vmem_limit_bytes=VMEM),
        cost_estimate=pl.CostEstimate(flops=flops, bytes_accessed=moved, transcendentals=exps),
    )


def array(shape, kind):
    return jax.ShapeDtypeStruct(tuple(shape), kind)


def whole(shape, **more):
    return pl.BlockSpec(tuple(shape), lambda step, place: (0,) * len(shape), **more)


def half_turn(values, cosine, sine):
    return values * cosine + pltpu.roll(values, HD // 2, 1) * sine


def heads_kernel(place, x, gain, cosine, sine, w_query, w_key, w_value, normed, blocks):
    step = pl.program_id(0)

    @pl.when(step == 0)
    def _():
        values = x[...].astype(F32)
        inverse = lax.rsqrt(jnp.mean(values * values, axis=-1, keepdims=True) + 1e-05)
        normed[...] = (values * inverse * gain[...]).astype(BF16)

    low = normed[...]
    count = w_query.shape[1] // HD
    for index, weight in enumerate((w_query, w_key, w_value)):
        part = dot(low, weight[...])
        for head in range(count):
            values = part[:, head * HD : (head + 1) * HD]
            if index < 2:
                values = half_turn(values, cosine[...], sine[...])
            spot = place[step * count + head]
            blocks[spot, :, index * HD : (index + 1) * HD] = values.astype(BF16)


def head_blocks(spots, x, gain, cosine, sine, w_query, w_key, w_value):
    rows, width = x.shape
    heads = w_query.shape[1] // HD
    weight = pl.BlockSpec((width, 2 * HD), lambda step, place: (0, step))
    blocks = (heads, rows, 3 * HD)
    return call(
        heads_kernel,
        spots,
        (heads // 2,),
        [whole((rows, width)), whole((1, width)), whole((rows, HD)), whole((rows, HD))]
        + [weight] * 3,
        [whole((rows, width)), whole(blocks)],
        [array((rows, width), BF16), array(blocks, BF16)],
        [],
        flops=6 * rows * width * heads * HD,
        moved=6 * width * heads * HD,
    )(spots, x, gain[None], cosine, sine, w_query, w_key, w_value)


def join_kernel(heads, place, mixed_grad, low, blocks):
    columns = low.shape[1] // heads
    for head in range(heads):
        blocks[place[head], :, :HD] = mixed_grad[:, head * HD : (head + 1) * HD]
        blocks[place[head], :, HD:] = low[:, head * columns : (head + 1) * columns]


def joined(spots, heads, mixed_grad, low):
    rows, width = low.shape
    blocks = (heads, rows, HD + width // heads)
    return call(
        functools.partial(join_kernel, heads),
        spots,
        (1,),
        [whole(mixed_grad.shape), whole(low.shape)],
        whole(blocks),
        array(blocks, BF16),
        [],
        moved=12 * rows * width,
    )(spots, mixed_grad, low)


def back_kernel(
    share, ring, place, received, pair, upstream, starts, places, cosine, sine,
    query_grad, own, other, total,
):
    heads, rows = received.shape[:2]
    core = place[2]
    group = 2 * share * rows
    scale = HD ** (-0.5)
    total[...] = jnp.zeros_like(total)
    for block, source in enumerate(ring):
        q, grad = received[block, :, :HD], upstream[block, :, :HD]
        start, spot = starts[block : block + 1], places[block : block + 1]
        sum_query = jnp.zeros((rows, HD), F32)
        for first in range(0, (source + 1) * group, KEYS):
            size = min(KEYS, (source + 1) * group - first)
            keys = pl.ds(first, size)
            k, v = pair[keys, :HD], pair[keys, HD:]
            scores = dot_back(k, q) * scale - math.log(BIAS_LEN)
            key_places = first + lax.broadcasted_iota(jnp.int32, (size, rows), 0)
            allowed = (key_places >= start) & (key_places <= spot)
            weights = jnp.where(allowed, jax.nn.sigmoid(scores), 0.0)
            total[keys, HD:] += dot(weights.astype(BF16), grad)
            score_grad = (dot_back(v, grad) * weights * (1.0 - weights)).astype(BF16)
            total[keys, :HD] += dot(score_grad, q) * scale
            sum_query += dot_rows(score_grad, k)
        query_grad[block] = half_turn(sum_query * scale, cosine[block], sine[block]).astype(BF16)
    both = total[...].reshape(heads * share, 2, rows, 2 * HD)
    mine, theirs = both[:, 0], both[:, 1]
    own[...] = jnp.where(core == 0, mine, theirs)
    other[...] = jnp.where(core == 0, theirs, mine).astype(BF16)


def attention_back(place, share, ring, received, pair, upstream, starts, places, cosine, sine):
    heads, rows = received.shape[:2]
    total = pair.shape[0]
    halves = (heads * share, rows, 2 * HD)
    block = (heads, rows, HD)
    return call(
        functools.partial(back_kernel, share, ring),
        place,
        (1,),
        [whole(received.shape), whole(pair.shape), whole(upstream.shape)]
        + [whole((heads, rows))] * 2
        + [whole(block)] * 2,
        [whole(block), whole(halves), whole(halves)],
        [array(block, BF16), array(halves, F32), array(halves, BF16)],
        [pltpu.VMEM((total, 2 * HD), F32)],
        flops=10 * heads * rows * total * HD // 2,
        moved=8 * total * HD,
        exps=heads * rows * total,
    )(place, received, pair, upstream, starts, places, cosine, sine)


def grads_kernel(ring, place, query_grad, own, received, cosine, sine, blocks):
    for index, source in enumerate(ring):
        both = own[source] + received[source].astype(F32)
        key = half_turn(both[:, :HD], cosine[index], sine[index])
        blocks[index, :, :HD] = query_grad[index]
        blocks[index, :, HD : 2 * HD] = key.astype(BF16)
        blocks[index, :, 2 * HD :] = both[:, HD:].astype(BF16)


def grad_blocks(place, ring, query_grad, own, received, cosine, sine):
    heads, rows = query_grad.shape[:2]
    block = (heads, rows, HD)
    blocks = (heads, rows, 3 * HD)
    return call(
        functools.partial(grads_kernel, ring),
        place,
        (1,),
        [whole(block), whole(own.shape), whole(received.shape), whole(block), whole(block)],
        whole(blocks),
        array(blocks, BF16),
        [],
        moved=20 * heads * rows * HD,
    )(place, query_grad, own, received, cosine, sine)


def project_back_kernel(ring, place, blocks, w_query, w_key, w_value, out, held):
    @pl.when(pl.program_id(0) == 0)
    def _():
        for index, head in enumerate(ring):
            for part in range(3):
                held[part, :, head * HD : (head + 1) * HD] = blocks[
                    index, :, part * HD : (part + 1) * HD
                ]

    out[...] = (
        dot_back(held[0], w_query[...])
        + dot_back(held[1], w_key[...])
        + dot_back(held[2], w_value[...])
    ).astype(BF16)


def projected_back(place, ring, blocks, w_query, w_key, w_value):
    rows = blocks.shape[1]
    width, local_width = w_query.shape
    weight = pl.BlockSpec((2 * TILE, local_width), lambda step, place: (step, 0))
    return call(
        functools.partial(project_back_kernel, ring),
        place,
        (width // (2 * TILE),),
        [whole(blocks.shape)] + [weight] * 3,
        pl.BlockSpec((rows, 2 * TILE), lambda step, place: (0, step)),
        array((rows, width), BF16),
        [pltpu.VMEM((3, rows, local_width), BF16)],
        flops=6 * rows * width * local_width,
        moved=6 * width * local_width,
    )(place, blocks, w_query, w_key, w_value)


def chip_kernel(
    half, own_normed, other_normed, hidden_grad, gate_w, up_w,
    back_own, back_other, hidden, normed, back_sum,
):
    step = pl.program_id(0)
    rows = own_normed.shape[0]

    @pl.when(step == 0)
    def _():
        normed[:rows] = own_normed[...]
        normed[rows:] = other_normed[...]
        back_sum[...] = jnp.zeros_like(back_sum)

    hidden[...], gate_low, upward_low = gated(
        normed[...], hidden_grad[...].astype(F32), gate_w[...], up_w[...]
    )
    back_sum[...] += dot_back(gate_low, gate_w[...]) + dot_back(upward_low, up_w[...])

    @pl.when(step == pl.num_programs(0) - 1)
    def _():
        back_own[...] = back_sum[:rows]
        back_other[...] = back_sum[rows:].astype(BF16)


def feed_kernel(half, hidden, weight, feed_own, feed_other):
    total = dot(hidden[...], weight[...])
    rows = feed_own.shape[0]
    feed_own[...] = total[:rows]
    feed_other[...] = total[rows:].astype(BF16)


def weight_specs(width, first, steps):
    def tile(step, place):
        return place[0] * steps + first + step

    columns = pl.BlockSpec((width, TILE), lambda step, place: (0, tile(step, place)))
    return [columns, columns, pl.BlockSpec((TILE, width), lambda step, place: (tile(step, place), 0))]


def chip_back(half, own_normed, other_normed, hidden_grad, weights):
    rows, width = own_normed.shape
    steps = weights[0].shape[1] // 2 // TILE
    block = whole((rows, width))
    tile = pl.BlockSpec((2 * rows, TILE), lambda step, place: (0, step))
    return call(
        chip_kernel,
        half,
        (steps,),
        [block] * 2 + [tile] + weight_specs(width, 0, steps)[:2],
        [block] * 2 + [tile],
        [
            array((rows, width), F32),
            array((rows, width), BF16),
            array((2 * rows, steps * TILE), BF16),
        ],
        [pltpu.VMEM((2 * rows, width), BF16), pltpu.VMEM((2 * rows, width), F32)],
        flops=16 * rows * width * steps * TILE,
        moved=4 * width * steps * TILE,
        exps=2 * rows * steps * TILE,
    )(half, own_normed, other_normed, hidden_grad, *weights[:2])


def chip_feed(half, hidden, w_down):
    tokens, units = hidden.shape
    width = w_down.shape[1]
    block = pl.BlockSpec((tokens // 2, 4 * TILE), lambda step, place: (0, step))
    return call(
        feed_kernel,
        half,
        (width // (4 * TILE),),
        [
            whole((tokens, units)),
            pl.BlockSpec((units, 4 * TILE), lambda step, place: (place[0], step)),
        ],
        [block] * 2,
        [array((tokens // 2, width), F32), array((tokens // 2, width), BF16)],
        [],
        flops=2 * tokens * width * units,
        moved=2 * width * units,
    )(half, hidden, w_down)


def plane_kernel(
    share, place, normed, normed_columns, grad_columns, hidden_grad, gate_w, up_w,
    kept, given, normed_turned, grad_turned, hidden, gate, upward,
):
    @pl.when(pl.program_id(0) == 0)
    def _():
        normed_turned[...] = normed_columns[...].T
        grad_turned[...] = grad_columns[...].T

    for first in range(0, normed.shape[0], TILE):
        rows = pl.ds(first, TILE)
        hidden[rows], gate[rows], upward[rows] = gated(
            normed[rows], hidden_grad[rows].astype(F32), gate_w[...], up_w[...]
        )
    core = place[2]
    for index, (left, right) in enumerate(
        ((normed_turned, gate), (normed_turned, upward), (grad_turned, hidden))
    ):
        both = dot(left[...], right[...]).reshape(2 * share, 2, -1, TILE)
        mine, theirs = both[:, 0].reshape(-1, TILE), both[:, 1].reshape(-1, TILE)
        kept[index] = jnp.where(core == 0, mine, theirs)
        given[index] = jnp.where(core == 0, theirs, mine).astype(BF16)


def plane_weight_grads(place, share, normed, grads, hidden_grad, weights, first, tiles):
    tokens, width = normed.shape
    steps = weights[0].shape[1] // 2 // TILE
    columns = width // 4
    out = pl.BlockSpec((3, columns // 2, TILE), lambda step, place: (0, 0, step))
    held = pl.BlockSpec((tokens, columns), lambda step, place: (0, place[1]))
    return call(
        functools.partial(plane_kernel, share),
        place,
        (tiles,),
        [
            whole((tokens, width), pipeline_mode=pl.Buffered(1)),
            held,
            held,
            pl.BlockSpec((tokens, TILE), lambda step, place: (0, step)),
        ]
        + weight_specs(width, first, steps)[:2],
        [out, out],
        [array((3, columns // 2, tiles * TILE), kind) for kind in (F32, BF16)],
        [pltpu.VMEM((columns, tokens), BF16)] * 2 + [pltpu.VMEM((tokens, TILE), BF16)] * 3,
        flops=2 * tokens * (2 * width + 3 * columns) * tiles * TILE,
        moved=4 * width * tiles * TILE,
        exps=tokens * tiles * TILE,
    )(place, normed, normed, grads, hidden_grad, *weights[:2])


def turn(out, mine, own, *others):
    @pl.when(mine)
    def _():
        out[...] = own[...].T

    @pl.when(jnp.logical_not(mine))
    def _():
        first = 0
        for other in others:
            out[:, first : first + other.shape[0]] = other[...].T
            first += other.shape[0]


def attention_weight_kernel(share, spots, place, own, other, grads, kept, given, turned):
    step = pl.program_id(0)
    turn(turned, step // (pl.num_programs(0) // 2) == place[4], own, other)
    both = dot(turned[...], grads[...]).reshape(2, share, 2, -1, grads.shape[1])
    for index in range(2):
        spot = place[spots + 2 * step + index]
        first = both[index, :, 0].reshape(kept.shape[1:])
        last = both[index, :, 1].reshape(kept.shape[1:])
        kept[spot] = jnp.where(place[2] == 0, first, last)
        given[spot] = jnp.where(place[2] == 0, last, first).astype(BF16)


def attention_weight_grads(place, share, heads, own, other, grads):
    tokens, half_width = own.shape
    tile, count = 4 * half_width // heads, heads // 4
    out = (heads, tile // 4, grads.shape[1])
    columns = pl.BlockSpec((tokens, tile), lambda step, place: (0, step % count))
    return call(
        functools.partial(attention_weight_kernel, share, place.shape[0] - heads),
        place,
        (heads // 2,),
        [columns, columns, whole(grads.shape)],
        [whole(out)] * 2,
        [array(out, F32), array(out, BF16)],
        [pltpu.VMEM((tile, tokens), BF16)],
        flops=4 * tokens * half_width * grads.shape[1],
        moved=8 * tokens * half_width,
    )(place, own, other, grads)


def attention_sums_kernel(ring, place, blocks, *refs):
    weights, sums, gain = refs[:3], refs[3:6], refs[6]
    total = jnp.zeros(gain.shape, F32)
    for index, head in enumerate(ring):
        columns = slice(head * HD, (head + 1) * HD)
        for part in range(3):
            grad = blocks[index, :, part * HD : (part + 1) * HD].astype(F32)
            sums[part][:, columns] = grad
            total += grad * weights[part][:, columns].astype(F32)
    gain[...] = total


def attention_sums(place, ring, blocks, weights):
    rows = blocks.shape[1]
    local_width = weights[0].shape[1]
    out = (rows, local_width)
    return call(
        functools.partial(attention_sums_kernel, ring),
        place,
        (1,),
        [whole(blocks.shape)] + [pl.BlockSpec(out, lambda step, place: (place[3], 0))] * 3,
        [whole(out)] * 3 + [whole((rows, HD))],
        [array(out, F32)] * 3 + [array((rows, HD), F32)],
        [],
        moved=24 * rows * local_width,
    )(place, blocks, *weights)


def feed_sums_kernel(count, place, *refs):
    pieces = refs[: 2 * count]
    gate_w, up_w, gate_sum, up_sum, down_sum, gain = refs[2 * count :]
    step = pl.program_id(0)

    @pl.when(step == 0)
    def _():
        gain[...] = jnp.zeros_like(gain)

    for index, piece in enumerate(pieces):

        @pl.when(step == index)
        def _(piece=piece):
            gate, up = piece[0].astype(F32), piece[1].astype(F32)
            gate_sum[...] = gate
            up_sum[...] = up
            down_sum[...] = piece[2].astype(F32).T
            terms = gate * gate_w[...].astype(F32) + up * up_w[...].astype(F32)
            total = gain[...]
            for first in range(0, terms.shape[1], HD):
                total += terms[:, first : first + HD]
            gain[...] = total


def feed_sums(place, sums, others, w_gate, w_up):
    count = len(sums)
    _, rows, units = others[0].shape
    hidden = w_gate.shape[1]

    def tile(step, place):
        return (place[0] ^ (step // count)) * count + step % count

    mine = pl.BlockSpec((3, None, rows, units), lambda step, place: (0, place[0], 0, 0))
    weight = pl.BlockSpec((rows, units), lambda step, place: (place[3], tile(step, place)))
    wide = pl.BlockSpec((rows, units), lambda step, place: (0, tile(step, place)))
    tall = pl.BlockSpec((units, rows), lambda step, place: (tile(step, place), 0))
    return call(
        functools.partial(feed_sums_kernel, count),
        place,
        (2 * count,),
        [mine] * count + [whole(others[0].shape)] * count + [weight] * 2,
        [wide, wide, tall, whole((rows, HD))],
        [
            array((rows, hidden), F32),
            array((rows, hidden), F32),
            array((hidden, rows), F32),
            array((rows, HD), F32),
        ],
        [],
        moved=34 * rows * hidden // 2,
    )(place, *sums, *others, w_gate, w_up)


def local(
    activations,
    doc_ids,
    w_query,
    w_key,
    w_value,
    w_out,
    w_gate,
    w_up,
    w_down,
    gain_attn,
    gain_mlp,
    cotangent,
):
    rows, width = activations.shape
    devices = lax.axis_size("seq")
    total = rows * devices
    features = width // devices
    local_width = w_query.shape[1]
    heads = local_width // HD
    share = devices // (2 * heads)
    me = lax.axis_index("seq")
    core = me % 2
    residue = (me // 2) % share
    head = me // (2 * share)
    tiles = w_gate.shape[1] // 2 // TILE
    feed_weights = (w_gate, w_up, w_down)

    def place(a, r, c):
        return (a * share + r) * 2 + c

    def split(s):
        return s // (2 * share), (s // 2) % share, s % 2

    def permuted(x, target):
        return lax.ppermute(x, "seq", [(s, target(*split(s))) for s in range(devices)])

    def core_swap(x):
        return permuted(x, lambda a, r, c: place(a, r, 1 - c))

    def pair_swap(x):
        return permuted(x, lambda a, r, c: place(a ^ 1, r, c))

    ring = (*range(0, heads, 2), *range(heads - 1, 0, -2))
    spots = [ring.index(a) for a in range(heads)]
    ring_groups = [[place(a, r, c) for a in ring] for r in range(share) for c in range(2)]

    def gathered(x):
        return lax.all_gather(x, "seq", axis=0, tiled=True, axis_index_groups=ring_groups)

    def head_swap(x):
        return lax.ppermute(x, "head", [(0, 1), (1, 0)])

    share_groups = [
        [place(a, r, c) for r in range(share)] for a in range(heads) for c in range(2)
    ]

    def after(x, *earlier):
        return lax.optimization_barrier((x, *earlier))[0]

    def exchange(x):
        return lax.all_to_all(x, "seq", 0, 0, tiled=True, axis_index_groups=ring_groups)

    def by_head(x):
        return jnp.stack([x[spot] for spot in spots])

    def share_sum(x, dim):
        if share == 1:
            return x
        return lax.psum_scatter(
            x, "seq", scatter_dimension=dim, tiled=True, axis_index_groups=share_groups
        )

    def in_core_order(mine, other, axis):
        return jnp.where(core == 0, jnp.stack([mine, other], axis), jnp.stack([other, mine], axis))

    def my_part(x, index, axis):
        return lax.dynamic_index_in_dim(x, index, axis, keepdims=False)

    column = lax.axis_index("head")

    def my_half(x):
        return lax.dynamic_slice_in_dim(x, column * (width // 2), width // 2, 1)

    last = []

    def following(x):
        return after(x, *last)

    def done(x):
        last[:] = [x]
        return x

    my_places = me * rows + jnp.arange(rows, dtype=jnp.int32)
    block_starts = place(jnp.array(ring, jnp.int32), residue, core) * rows
    query_places = block_starts[:, None] + jnp.arange(rows, dtype=jnp.int32)[None, :]
    query_docs = doc_ids.reshape(heads, share, 2, rows)[jnp.array(ring), residue, core]
    query_starts = jnp.sum((doc_ids < query_docs[..., None]).astype(jnp.int32), -1)
    key_places = jnp.arange(total, dtype=jnp.int32)
    allowed = (key_places >= query_starts.reshape(-1, 1)) & (
        key_places <= query_places.reshape(-1, 1)
    )
    scale = HD ** (-0.5)
    core_index = core[None].astype(jnp.int32)
    spot_index = jnp.array(spots, jnp.int32)
    position = jnp.concatenate([jnp.stack([head % 2, head // 2, core, me, column]), spot_index]).astype(jnp.int32)

    plane_cotangent = gathered(cotangent)
    inputs = activations.astype(F32)
    cosine, sine = turning(my_places, 1.0)
    normed_low, blocks = head_blocks(
        spot_index, activations, gain_attn, cosine, sine, w_query, w_key, w_value
    )
    chip_cotangent = jnp.concatenate([cotangent, core_swap(cotangent)], 0)
    half_tiles = tiles // 2
    down_quarters = w_down.reshape(4, -1, width)

    def hidden_grads(grads, half, part):
        return dot_back(grads, my_part(down_quarters, 2 * half + part, 0)).astype(BF16)

    chip_grads = after(chip_cotangent, blocks)
    chip_hidden_grad = jnp.concatenate([hidden_grads(chip_grads, core, part) for part in range(2)], 1)
    head_rows = after(exchange(blocks), chip_hidden_grad)

    def all_keys(own):
        if share > 1:
            own = lax.all_gather(own, "seq", axis=1, axis_index_groups=share_groups)
        else:
            own = own[:, None]
        return in_core_order(own, core_swap(own), 2).reshape(total, 2 * HD)

    head_kv = all_keys(by_head(head_rows[:, :, HD:]))
    scores = dot_back(head_rows[:, :, :HD].reshape(heads * rows, HD), head_kv[:, :HD])
    weights = jnp.where(allowed, jax.nn.sigmoid(scores * scale - math.log(BIAS_LEN)), 0.0)
    head_mixed = dot(weights.astype(BF16), head_kv[:, HD:]).astype(BF16)
    attended = by_head(exchange(head_mixed.reshape(heads, rows, HD)))
    attended = attended.transpose(1, 0, 2).reshape(rows, -1)

    branch = dot(attended, w_out).astype(BF16)
    branch_received = head_swap(branch)
    cosines, sines = turning(after(query_places, branch), -1.0)
    first_hidden_grad = hidden_grads(after(plane_cotangent, branch, cosines, sines), head % 2, 0)
    branch_received = after(branch_received, first_hidden_grad)
    middle = inputs + (branch.astype(F32) + branch_received.astype(F32))
    second, _ = normalized(middle, gain_mlp)
    second_low = second.astype(BF16)
    plane_second = gathered(second_low)

    back_own, back_other, hidden = chip_back(
        core_index, second_low, core_swap(second_low), chip_hidden_grad, feed_weights
    )

    def core_sum(own, other):
        return (own + core_swap(other).astype(F32)).astype(BF16)

    back_low = core_sum(back_own, back_other)
    back_received = head_swap(back_low)
    done(back_low)
    last_hidden_grad = done(hidden_grads(following(plane_cotangent), head % 2, 1))
    feed_own, feed_other = chip_feed(core_index, following(hidden), w_down)
    done(feed_own)
    upstream = back_low.astype(F32) + following(back_received).astype(F32)
    inverse = lax.rsqrt(jnp.mean(middle * middle, axis=-1, keepdims=True) + 1e-05)
    middle_grad = cotangent.astype(F32) + norm_back(middle, inverse, gain_mlp, upstream)
    branch_low = middle_grad.astype(BF16)
    blocks = joined(spot_index, heads, dot_back(branch_low, w_out).astype(BF16), branch_low)
    done(blocks)
    own_normed = gathered(following(my_half(normed_low)))
    other_normed = head_swap(own_normed)
    upstream = exchange(blocks)
    feed_low = done(core_sum(following(feed_own), feed_other))
    feed_received = head_swap(feed_low)

    def plane_piece(first, hidden_grad):
        kept, given = plane_weight_grads(
            position,
            share,
            following(plane_second),
            plane_cotangent,
            hidden_grad,
            feed_weights,
            first,
            half_tiles,
        )
        done(given)
        return kept, core_swap(given)

    def plane_halves(kept, received):
        sums = following(kept) + received.astype(F32)
        sums = share_sum(sums.reshape(6, share, features, -1), 1).reshape(3, 2, features, -1)
        sums = done(sums.astype(BF16))
        return sums, pair_swap(done(my_part(sums, 1 - head % 2, 1)))

    first_piece = plane_piece(0, first_hidden_grad)
    feed = following(feed_low).astype(F32) + feed_received.astype(F32)
    output = done((middle + feed).astype(BF16))
    upstream = following(upstream)
    query_grad, own_grad, other_grad = attention_back(
        position,
        share,
        ring,
        head_rows,
        head_kv,
        upstream,
        query_starts,
        query_places,
        cosines,
        sines,
    )
    done(other_grad)
    all_attended = gathered(following(attended))
    received = core_swap(other_grad)
    if share > 1:
        shape = (heads, share, rows, 2 * HD)
        own_grad = share_sum((own_grad + received.astype(F32)).reshape(shape), 1)[:, 0]
        received = jnp.zeros(own_grad.shape, BF16)
    ring_grads = done(
        grad_blocks(position, ring, following(query_grad), own_grad, received, cosines, sines)
    )
    received = exchange(ring_grads)
    first_halves = plane_halves(*first_piece)
    last_piece = plane_piece(half_tiles, last_hidden_grad)

    normed_part = done(projected_back(position, ring, following(received), w_query, w_key, w_value))
    normed_received = head_swap(normed_part)
    own_sum, other_sum = attention_weight_grads(
        position,
        share,
        heads,
        own_normed,
        other_normed,
        following(ring_grads).reshape(heads * rows, -1),
    )
    done(other_sum)
    other_received = core_swap(other_sum)
    if share > 1:
        own_sum = (own_sum + other_received.astype(F32)).reshape(heads, share, features, -1)
        own_sum = share_sum(own_sum, 1)[:, 0]
        other_received = jnp.zeros(own_sum.shape, BF16)
    sum_received = exchange(done((following(own_sum) + other_received.astype(F32)).astype(BF16)))
    last_halves = plane_halves(*last_piece)
    out_part = done(dot_rows(following(all_attended), following(upstream)[:, :, HD:].reshape(heads * rows, -1)))
    out_part = out_part.reshape(local_width, share, 2, features)
    out_given = done(my_part(out_part, 1 - core, 2).astype(BF16))
    out_sum = my_part(out_part, core, 2) + core_swap(out_given).astype(F32)
    out_sum = share_sum(out_sum, 1).reshape(local_width, features)
    normed_grad = following(normed_part).astype(F32) + normed_received.astype(F32)
    inverse_attn = lax.rsqrt(jnp.mean(inputs * inputs, axis=-1, keepdims=True) + 1e-05)
    input_grad = (middle_grad + norm_back(inputs, inverse_attn, gain_attn, normed_grad)).astype(BF16)
    done(input_grad)

    query_sum, key_sum, value_sum, attention_gain = attention_sums(
        position,
        ring,
        following(sum_received),
        (w_query, w_key, w_value),
    )
    done(attention_gain)
    gate_sum, up_sum, down_sum, feed_gain = feed_sums(
        position,
        [following(first_halves[0]), last_halves[0]],
        [first_halves[1], last_halves[1]],
        w_gate,
        w_up,
    )

    def gain_sum(terms, gain):
        return jnp.sum(terms, axis=1) / lax.dynamic_slice_in_dim(gain, me * features, features, 0)

    gains = jnp.stack([gain_sum(attention_gain, gain_attn), gain_sum(feed_gain, gain_mlp)])
    gains = gains + head_swap(gains)
    return (
        output,
        input_grad,
        query_sum,
        key_sum,
        value_sum,
        out_sum,
        gate_sum,
        up_sum,
        down_sum,
        gains[0],
        gains[1],
    )


def solution(mesh):
    placed = (
        P("seq", None),
        P(),
        P(None, "head"),
        P(None, "head"),
        P(None, "head"),
        P("head", None),
        P(None, "head"),
        P(None, "head"),
        P("head", None),
        P(),
        P(),
        P("seq", None),
    )
    return jax.shard_map(
        local,
        mesh=mesh,
        in_specs=placed,
        out_specs=(
            P("seq", None),
            P("seq", None),
            P("seq", "head"),
            P("seq", "head"),
            P("seq", "head"),
            P("head", "seq"),
            P("seq", "head"),
            P("seq", "head"),
            P("head", "seq"),
            P("seq"),
            P("seq"),
        ),
        check_vma=False,
    )
```

```python
import functools
import math

import jax
import jax.numpy as jnp
from jax import lax
from jax.experimental import pallas as pl
from jax.experimental.pallas import tpu as pltpu
from jax.sharding import PartitionSpec as P

HD = 128
BIAS_LEN = 4096
BF16 = jnp.bfloat16
F32 = jnp.float32
TILE = 256
KEYS = 1024
VMEM = 60 * 1024 * 1024


def frequencies(head_dim):
    half_dim = head_dim // 2
    return jnp.exp(-jnp.arange(half_dim).astype(F32) * (2.0 / head_dim) * math.log(10000.0))


def turning(places, sign):
    angles = places.astype(F32)[..., None] * frequencies(HD)
    cosine, sine = jnp.cos(angles), sign * jnp.sin(angles)
    return jnp.concatenate([cosine, cosine], -1), jnp.concatenate([-sine, sine], -1)


def normalized(values, gain):
    inverse = lax.rsqrt(jnp.mean(values * values, axis=-1, keepdims=True) + 1e-05)
    return values * inverse * gain, inverse


def norm_back(values, inverse, gain, upstream):
    scaled = values * inverse
    weighted = upstream * gain
    return inverse * (weighted - scaled * jnp.mean(weighted * scaled, axis=-1, keepdims=True))


def dot(one, two):
    return jnp.dot(one, two, preferred_element_type=F32)


def dot_rows(one, two):
    return lax.dot_general(one, two, (((0,), (0,)), ((), ())), preferred_element_type=F32)


def dot_back(one, two):
    return lax.dot_general(one, two, (((1,), (1,)), ((), ())), preferred_element_type=F32)


def gated(normed, hidden_grad, gate_w, up_w):
    gate = dot(normed, gate_w)
    upward = dot(normed, up_w)
    gate_sig = jax.nn.sigmoid(gate)
    silu = gate * gate_sig
    hidden_low = (silu * upward).astype(BF16)
    gate_low = (hidden_grad * upward * (gate_sig + silu * (1.0 - gate_sig))).astype(BF16)
    upward_low = (hidden_grad * silu).astype(BF16)
    return hidden_low, gate_low, upward_low


def call(kernel, scalars, grid, in_specs, out_specs, shapes, scratch, flops=0, moved=0, exps=0):
    return pl.pallas_call(
        kernel,
        grid_spec=pltpu.PrefetchScalarGridSpec(
            num_scalar_prefetch=1,
            grid=grid,
            in_specs=in_specs,
            out_specs=out_specs,
            scratch_shapes=scratch,
        ),
        out_shape=shapes,
        compiler_params=pltpu.CompilerParams(vmem_limit_bytes=VMEM),
        cost_estimate=pl.CostEstimate(flops=flops, bytes_accessed=moved, transcendentals=exps),
    )


def array(shape, kind):
    return jax.ShapeDtypeStruct(tuple(shape), kind)


def whole(shape, **more):
    return pl.BlockSpec(tuple(shape), lambda step, place: (0,) * len(shape), **more)


def half_turn(values, cosine, sine):
    return values * cosine + pltpu.roll(values, HD // 2, 1) * sine


def heads_kernel(place, x, gain, cosine, sine, w_query, w_key, w_value, normed, blocks):
    step = pl.program_id(0)

    @pl.when(step == 0)
    def _():
        values = x[...].astype(F32)
        inverse = lax.rsqrt(jnp.mean(values * values, axis=-1, keepdims=True) + 1e-05)
        normed[...] = (values * inverse * gain[...]).astype(BF16)

    low = normed[...]
    count = w_query.shape[1] // HD
    for index, weight in enumerate((w_query, w_key, w_value)):
        part = dot(low, weight[...])
        for head in range(count):
            values = part[:, head * HD : (head + 1) * HD]
            if index < 2:
                values = half_turn(values, cosine[...], sine[...])
            spot = place[step * count + head]
            blocks[spot, :, index * HD : (index + 1) * HD] = values.astype(BF16)


def head_blocks(spots, x, gain, cosine, sine, w_query, w_key, w_value):
    rows, width = x.shape
    heads = w_query.shape[1] // HD
    weight = pl.BlockSpec((width, 4 * HD), lambda step, place: (0, step))
    blocks = (heads, rows, 3 * HD)
    return call(
        heads_kernel,
        spots,
        (heads // 4,),
        [whole((rows, width)), whole((1, width)), whole((rows, HD)), whole((rows, HD))]
        + [weight] * 3,
        [whole((rows, width)), whole(blocks)],
        [array((rows, width), BF16), array(blocks, BF16)],
        [],
        flops=36 * rows * width * heads * HD,
        moved=6 * width * heads * HD,
    )(spots, x, gain[None], cosine, sine, w_query, w_key, w_value)


def join_kernel(heads, place, mixed_grad, low, blocks):
    columns = low.shape[1] // heads
    for head in range(heads):
        blocks[place[head], :, :HD] = mixed_grad[:, head * HD : (head + 1) * HD]
        blocks[place[head], :, HD:] = low[:, head * columns : (head + 1) * columns]


def joined(spots, heads, mixed_grad, low):
    rows, width = low.shape
    blocks = (heads, rows, HD + width // heads)
    return call(
        functools.partial(join_kernel, heads),
        spots,
        (1,),
        [whole(mixed_grad.shape), whole(low.shape)],
        whole(blocks),
        array(blocks, BF16),
        [],
        moved=40 * rows * width,
    )(spots, mixed_grad, low)


def back_kernel(
    share, ring, place, received, pair, upstream, starts, places, cosine, sine,
    query_grad, own, other, total,
):
    heads, rows = received.shape[:2]
    core = place[2]
    group = 2 * share * rows
    scale = HD ** (-0.5)
    total[...] = jnp.zeros_like(total)
    for block, source in enumerate(ring):
        q, grad = received[block, :, :HD], upstream[block, :, :HD]
        start, spot = starts[block : block + 1], places[block : block + 1]
        sum_query = jnp.zeros((rows, HD), F32)
        for first in range(0, (source + 1) * group, KEYS):
            size = min(KEYS, (source + 1) * group - first)
            keys = pl.ds(first, size)
            k, v = pair[keys, :HD], pair[keys, HD:]
            scores = dot_back(k, q) * scale - math.log(BIAS_LEN)
            key_places = first + lax.broadcasted_iota(jnp.int32, (size, rows), 0)
            allowed = (key_places >= start) & (key_places <= spot)
            weights = jnp.where(allowed, jax.nn.sigmoid(scores), 0.0)
            total[keys, HD:] += dot(weights.astype(BF16), grad)
            score_grad = (dot_back(v, grad) * weights * (1.0 - weights)).astype(BF16)
            total[keys, :HD] += dot(score_grad, q) * scale
            sum_query += dot_rows(score_grad, k)
        query_grad[block] = half_turn(sum_query * scale, cosine[block], sine[block]).astype(BF16)
    both = total[...].reshape(heads * share, 2, rows, 2 * HD)
    mine, theirs = both[:, 0], both[:, 1]
    own[...] = jnp.where(core == 0, mine, theirs)
    other[...] = jnp.where(core == 0, theirs, mine).astype(BF16)


def attention_back(place, share, ring, received, pair, upstream, starts, places, cosine, sine):
    heads, rows = received.shape[:2]
    total = pair.shape[0]
    halves = (heads * share, rows, 2 * HD)
    block = (heads, rows, HD)
    return call(
        functools.partial(back_kernel, share, ring),
        place,
        (1,),
        [whole(received.shape), whole(pair.shape), whole(upstream.shape)]
        + [whole((heads, rows))] * 2
        + [whole(block)] * 2,
        [whole(block), whole(halves), whole(halves)],
        [array(block, BF16), array(halves, F32), array(halves, BF16)],
        [pltpu.VMEM((total, 2 * HD), F32)],
        flops=36 * heads * rows * total * HD,
        moved=8 * total * HD,
        exps=heads * rows * total,
    )(place, received, pair, upstream, starts, places, cosine, sine)


def grads_kernel(ring, place, query_grad, own, received, cosine, sine, blocks):
    for index, source in enumerate(ring):
        both = own[source] + received[source].astype(F32)
        key = half_turn(both[:, :HD], cosine[index], sine[index])
        blocks[index, :, :HD] = query_grad[index]
        blocks[index, :, HD : 2 * HD] = key.astype(BF16)
        blocks[index, :, 2 * HD :] = both[:, HD:].astype(BF16)


def grad_blocks(place, ring, query_grad, own, received, cosine, sine):
    heads, rows = query_grad.shape[:2]
    block = (heads, rows, HD)
    blocks = (heads, rows, 3 * HD)
    return call(
        functools.partial(grads_kernel, ring),
        place,
        (1,),
        [whole(block), whole(own.shape), whole(received.shape), whole(block), whole(block)],
        whole(blocks),
        array(blocks, BF16),
        [],
        moved=90 * heads * rows * HD,
    )(place, query_grad, own, received, cosine, sine)


def project_back_kernel(ring, place, blocks, w_query, w_key, w_value, out, held):
    @pl.when(pl.program_id(0) == 0)
    def _():
        for index, head in enumerate(ring):
            for part in range(3):
                held[part, :, head * HD : (head + 1) * HD] = blocks[
                    index, :, part * HD : (part + 1) * HD
                ]

    out[...] = (
        dot_back(held[0], w_query[...])
        + dot_back(held[1], w_key[...])
        + dot_back(held[2], w_value[...])
    ).astype(BF16)


def projected_back(place, ring, blocks, w_query, w_key, w_value):
    rows = blocks.shape[1]
    width, local_width = w_query.shape
    weight = pl.BlockSpec((4 * TILE, local_width), lambda step, place: (step, 0))
    return call(
        functools.partial(project_back_kernel, ring),
        place,
        (width // (4 * TILE),),
        [whole(blocks.shape)] + [weight] * 3,
        pl.BlockSpec((rows, 4 * TILE), lambda step, place: (0, step)),
        array((rows, width), BF16),
        [pltpu.VMEM((3, rows, local_width), BF16)],
        flops=42 * rows * width * local_width,
        moved=6 * width * local_width,
    )(place, blocks, w_query, w_key, w_value)


def chip_kernel(
    half, own_normed, other_normed, hidden_grad, gate_w, up_w,
    back_own, back_other, hidden, normed, back_sum,
):
    step = pl.program_id(0)
    rows = own_normed.shape[0]

    @pl.when(step == 0)
    def _():
        normed[:rows] = own_normed[...]
        normed[rows:] = other_normed[...]
        back_sum[...] = jnp.zeros_like(back_sum)

    hidden[...], gate_low, upward_low = gated(
        normed[...], hidden_grad[...].astype(F32), gate_w[...], up_w[...]
    )
    back_sum[...] += dot_back(gate_low, gate_w[...]) + dot_back(upward_low, up_w[...])

    @pl.when(step == pl.num_programs(0) - 1)
    def _():
        back_own[...] = back_sum[:rows]
        back_other[...] = back_sum[rows:].astype(BF16)


def feed_kernel(half, hidden, weight, feed_own, feed_other):
    total = dot(hidden[...], weight[...])
    rows = feed_own.shape[0]
    feed_own[...] = total[:rows]
    feed_other[...] = total[rows:].astype(BF16)


def weight_specs(width, first, steps):
    def tile(step, place):
        return place[0] * steps + first + step

    columns = pl.BlockSpec((width, TILE), lambda step, place: (0, tile(step, place)))
    return [columns, columns, pl.BlockSpec((TILE, width), lambda step, place: (tile(step, place), 0))]


def chip_back(half, own_normed, other_normed, hidden_grad, weights):
    rows, width = own_normed.shape
    steps = weights[0].shape[1] // 2 // TILE
    block = whole((rows, width))
    tile = pl.BlockSpec((2 * rows, TILE), lambda step, place: (0, step))
    return call(
        chip_kernel,
        half,
        (steps,),
        [block] * 2 + [tile] + weight_specs(width, 0, steps)[:2],
        [block] * 2 + [tile],
        [
            array((rows, width), F32),
            array((rows, width), BF16),
            array((2 * rows, steps * TILE), BF16),
        ],
        [pltpu.VMEM((2 * rows, width), BF16), pltpu.VMEM((2 * rows, width), F32)],
        flops=34 * rows * width * steps * TILE,
        moved=4 * width * steps * TILE,
        exps=2 * rows * steps * TILE,
    )(half, own_normed, other_normed, hidden_grad, *weights[:2])


def chip_feed(half, hidden, w_down):
    tokens, units = hidden.shape
    width = w_down.shape[1]
    block = pl.BlockSpec((tokens // 2, 4 * TILE), lambda step, place: (0, step))
    return call(
        feed_kernel,
        half,
        (width // (4 * TILE),),
        [
            whole((tokens, units)),
            pl.BlockSpec((units, 4 * TILE), lambda step, place: (place[0], step)),
        ],
        [block] * 2,
        [array((tokens // 2, width), F32), array((tokens // 2, width), BF16)],
        [],
        flops=6 * tokens * width * units,
        moved=2 * width * units,
    )(half, hidden, w_down)


def plane_kernel(
    share, place, normed, normed_columns, grad_columns, hidden_grad, gate_w, up_w,
    kept, given, normed_turned, grad_turned, hidden, gate, upward,
):
    @pl.when(pl.program_id(0) == 0)
    def _():
        normed_turned[...] = normed_columns[...].T
        grad_turned[...] = grad_columns[...].T

    for first in range(0, normed.shape[0], TILE):
        rows = pl.ds(first, TILE)
        hidden[rows], gate[rows], upward[rows] = gated(
            normed[rows], hidden_grad[rows].astype(F32), gate_w[...], up_w[...]
        )
    core = place[2]
    for index, (left, right) in enumerate(
        ((normed_turned, gate), (normed_turned, upward), (grad_turned, hidden))
    ):
        both = dot(left[...], right[...]).reshape(2 * share, 2, -1, TILE)
        mine, theirs = both[:, 0].reshape(-1, TILE), both[:, 1].reshape(-1, TILE)
        kept[index] = jnp.where(core == 0, mine, theirs)
        given[index] = jnp.where(core == 0, theirs, mine).astype(BF16)


def plane_weight_grads(place, share, normed, grads, hidden_grad, weights, first, tiles):
    tokens, width = normed.shape
    steps = weights[0].shape[1] // 2 // TILE
    columns = width // 4
    out = pl.BlockSpec((3, columns // 2, TILE), lambda step, place: (0, 0, step))
    held = pl.BlockSpec((tokens, columns), lambda step, place: (0, place[1]))
    return call(
        functools.partial(plane_kernel, share),
        place,
        (tiles,),
        [
            whole((tokens, width), pipeline_mode=pl.Buffered(1)),
            held,
            held,
            pl.BlockSpec((tokens, TILE), lambda step, place: (0, step)),
        ]
        + weight_specs(width, first, steps)[:2],
        [out, out],
        [array((3, columns // 2, tiles * TILE), kind) for kind in (F32, BF16)],
        [pltpu.VMEM((columns, tokens), BF16)] * 2 + [pltpu.VMEM((tokens, TILE), BF16)] * 3,
        flops=4 * tokens * (2 * width + 3 * columns) * tiles * TILE,
        moved=4 * width * tiles * TILE,
        exps=tokens * tiles * TILE,
    )(place, normed, normed, grads, hidden_grad, *weights[:2])


def turn(out, mine, own, *others):
    @pl.when(mine)
    def _():
        out[...] = own[...].T

    @pl.when(jnp.logical_not(mine))
    def _():
        first = 0
        for other in others:
            out[:, first : first + other.shape[0]] = other[...].T
            first += other.shape[0]


def attention_weight_kernel(share, spots, place, own, other, grads, kept, given, turned):
    step = pl.program_id(0)
    turn(turned, step // (pl.num_programs(0) // 2) == place[4], own, other)
    both = dot(turned[...], grads[...]).reshape(2, share, 2, -1, grads.shape[1])
    for index in range(2):
        spot = place[spots + 2 * step + index]
        first = both[index, :, 0].reshape(kept.shape[1:])
        last = both[index, :, 1].reshape(kept.shape[1:])
        kept[spot] = jnp.where(place[2] == 0, first, last)
        given[spot] = jnp.where(place[2] == 0, last, first).astype(BF16)


def attention_weight_grads(place, share, heads, own, other, grads):
    tokens, half_width = own.shape
    tile, count = 4 * half_width // heads, heads // 4
    out = (heads, tile // 4, grads.shape[1])
    columns = pl.BlockSpec((tokens, tile), lambda step, place: (0, step % count))
    return call(
        functools.partial(attention_weight_kernel, share, place.shape[0] - heads),
        place,
        (heads // 2,),
        [columns, columns, whole(grads.shape)],
        [whole(out)] * 2,
        [array(out, F32), array(out, BF16)],
        [pltpu.VMEM((tile, tokens), BF16)],
        flops=12 * tokens * half_width * grads.shape[1],
        moved=8 * tokens * half_width,
    )(place, own, other, grads)


def attention_sums_kernel(ring, place, blocks, *refs):
    weights, sums, gain = refs[:3], refs[3:6], refs[6]
    total = jnp.zeros(gain.shape, F32)
    for index, head in enumerate(ring):
        columns = slice(head * HD, (head + 1) * HD)
        for part in range(3):
            grad = blocks[index, :, part * HD : (part + 1) * HD].astype(F32)
            sums[part][:, columns] = grad
            total += grad * weights[part][:, columns].astype(F32)
    gain[...] = total


def attention_sums(place, ring, blocks, weights):
    rows = blocks.shape[1]
    local_width = weights[0].shape[1]
    out = (rows, local_width)
    return call(
        functools.partial(attention_sums_kernel, ring),
        place,
        (1,),
        [whole(blocks.shape)] + [pl.BlockSpec(out, lambda step, place: (place[3], 0))] * 3,
        [whole(out)] * 3 + [whole((rows, HD))],
        [array(out, F32)] * 3 + [array((rows, HD), F32)],
        [],
        moved=90 * rows * local_width,
    )(place, blocks, *weights)


def feed_sums_kernel(count, place, *refs):
    pieces = refs[:count], refs[count : 2 * count]
    gate_w, up_w, gate_sum, up_sum, down_sum, gain = refs[2 * count :]
    step = pl.program_id(0)

    @pl.when(step == 0)
    def _():
        gain[...] = jnp.zeros_like(gain)

    for source in range(2):

        @pl.when(step == source)
        def _(source=source):
            total = gain[...]
            first = 0
            for piece in pieces[source]:
                columns = slice(first, first + piece.shape[-1])
                first = columns.stop
                gate, up = piece[0].astype(F32), piece[1].astype(F32)
                gate_sum[:, columns] = gate
                up_sum[:, columns] = up
                down_sum[columns] = piece[2].astype(F32).T
                terms = gate * gate_w[:, columns].astype(F32) + up * up_w[:, columns].astype(F32)
                for spot in range(0, terms.shape[1], HD):
                    total += terms[:, spot : spot + HD]
            gain[...] = total


def feed_sums(place, sums, others, w_gate, w_up):
    rows = others[0].shape[1]
    hidden = w_gate.shape[1]

    def half(step, place):
        return place[0] ^ step

    def mine(piece):
        shape = (3, None, rows, piece.shape[-1])
        return pl.BlockSpec(shape, lambda step, place: (0, place[0], 0, 0))

    weight = pl.BlockSpec((rows, hidden // 2), lambda step, place: (place[3], half(step, place)))
    wide = pl.BlockSpec((rows, hidden // 2), lambda step, place: (0, half(step, place)))
    tall = pl.BlockSpec((hidden // 2, rows), lambda step, place: (half(step, place), 0))
    return call(
        functools.partial(feed_sums_kernel, len(sums)),
        place,
        (2,),
        [mine(piece) for piece in sums] + [whole(piece.shape) for piece in others] + [weight] * 2,
        [wide, wide, tall, whole((rows, HD))],
        [
            array((rows, hidden), F32),
            array((rows, hidden), F32),
            array((hidden, rows), F32),
            array((rows, HD), F32),
        ],
        [],
        moved=45 * rows * hidden,
    )(place, *sums, *others, w_gate, w_up)


def local(
    activations,
    doc_ids,
    w_query,
    w_key,
    w_value,
    w_out,
    w_gate,
    w_up,
    w_down,
    gain_attn,
    gain_mlp,
    cotangent,
):
    rows, width = activations.shape
    devices = lax.axis_size("seq")
    total = rows * devices
    features = width // devices
    local_width = w_query.shape[1]
    heads = local_width // HD
    share = devices // (2 * heads)
    me = lax.axis_index("seq")
    core = me % 2
    residue = (me // 2) % share
    head = me // (2 * share)
    tiles = w_gate.shape[1] // 2 // TILE
    feed_weights = (w_gate, w_up, w_down)

    def place(a, r, c):
        return (a * share + r) * 2 + c

    def split(s):
        return s // (2 * share), (s // 2) % share, s % 2

    def permuted(x, target):
        return lax.ppermute(x, "seq", [(s, target(*split(s))) for s in range(devices)])

    def core_swap(x):
        return permuted(x, lambda a, r, c: place(a, r, 1 - c))

    def pair_swap(x):
        return permuted(x, lambda a, r, c: place(a ^ 1, r, c))

    ring = (*range(0, heads, 2), *range(heads - 1, 0, -2))
    spots = [ring.index(a) for a in range(heads)]
    ring_groups = [[place(a, r, c) for a in ring] for r in range(share) for c in range(2)]

    def gathered(x):
        return lax.all_gather(x, "seq", axis=0, tiled=True, axis_index_groups=ring_groups)

    def head_swap(x):
        return lax.ppermute(x, "head", [(0, 1), (1, 0)])

    share_groups = [
        [place(a, r, c) for r in range(share)] for a in range(heads) for c in range(2)
    ]

    def after(x, *earlier):
        return lax.optimization_barrier((x, *earlier))[0]

    def exchange(x):
        return lax.all_to_all(x, "seq", 0, 0, tiled=True, axis_index_groups=ring_groups)

    def by_head(x):
        return jnp.stack([x[spot] for spot in spots])

    def share_sum(x, dim):
        if share == 1:
            return x
        return lax.psum_scatter(
            x, "seq", scatter_dimension=dim, tiled=True, axis_index_groups=share_groups
        )

    def in_core_order(mine, other, axis):
        return jnp.where(core == 0, jnp.stack([mine, other], axis), jnp.stack([other, mine], axis))

    def my_part(x, index, axis):
        return lax.dynamic_index_in_dim(x, index, axis, keepdims=False)

    column = lax.axis_index("head")

    def my_half(x):
        return lax.dynamic_slice_in_dim(x, column * (width // 2), width // 2, 1)

    last = []

    def following(x):
        return after(x, *last)

    def done(x):
        last[:] = [x]
        return x

    my_places = me * rows + jnp.arange(rows, dtype=jnp.int32)
    block_starts = place(jnp.array(ring, jnp.int32), residue, core) * rows
    query_places = block_starts[:, None] + jnp.arange(rows, dtype=jnp.int32)[None, :]
    query_docs = doc_ids.reshape(heads, share, 2, rows)[jnp.array(ring), residue, core]
    query_starts = jnp.sum((doc_ids < query_docs[..., None]).astype(jnp.int32), -1)
    key_places = jnp.arange(total, dtype=jnp.int32)
    allowed = (key_places >= query_starts.reshape(-1, 1)) & (
        key_places <= query_places.reshape(-1, 1)
    )
    scale = HD ** (-0.5)
    core_index = core[None].astype(jnp.int32)
    spot_index = jnp.array(spots, jnp.int32)
    position = jnp.concatenate([jnp.stack([head % 2, head // 2, core, me, column]), spot_index]).astype(jnp.int32)

    plane_cotangent = gathered(cotangent)
    inputs = activations.astype(F32)
    cosine, sine = turning(my_places, 1.0)
    normed_low, blocks = head_blocks(
        spot_index, activations, gain_attn, cosine, sine, w_query, w_key, w_value
    )
    chip_cotangent = jnp.concatenate([cotangent, core_swap(cotangent)], 0)
    early_tiles = tiles * 4 // 8
    late_tiles = tiles - early_tiles
    def hidden_grads(grads, half, first, count):
        start = (half * tiles + first) * TILE
        return dot_back(grads, lax.dynamic_slice_in_dim(w_down, start, count * TILE, 0)).astype(BF16)

    chip_grads = after(chip_cotangent, blocks)
    chip_hidden_grad = hidden_grads(chip_grads, core, 0, tiles)
    head_rows = after(exchange(blocks), chip_hidden_grad)

    def all_keys(own):
        if share > 1:
            own = lax.all_gather(own, "seq", axis=1, axis_index_groups=share_groups)
        else:
            own = own[:, None]
        return in_core_order(own, core_swap(own), 2).reshape(total, 2 * HD)

    head_kv = all_keys(by_head(head_rows[:, :, HD:]))
    scores = dot_back(head_rows[:, :, :HD].reshape(heads * rows, HD), head_kv[:, :HD])
    weights = jnp.where(allowed, jax.nn.sigmoid(scores * scale - math.log(BIAS_LEN)), 0.0)
    head_mixed = dot(weights.astype(BF16), head_kv[:, HD:]).astype(BF16)
    attended = by_head(exchange(head_mixed.reshape(heads, rows, HD)))
    attended = attended.transpose(1, 0, 2).reshape(rows, -1)

    branch = dot(attended, w_out).astype(BF16)
    branch_received = head_swap(branch)
    cosines, sines = turning(after(query_places, branch), -1.0)
    first_hidden_grad = hidden_grads(
        after(plane_cotangent, branch, cosines, sines), head % 2, 0, early_tiles
    )
    branch_received = after(branch_received, first_hidden_grad)
    middle = inputs + (branch.astype(F32) + branch_received.astype(F32))
    second, _ = normalized(middle, gain_mlp)
    second_low = second.astype(BF16)
    plane_second = gathered(second_low)

    back_own, back_other, hidden = chip_back(
        core_index, second_low, core_swap(second_low), chip_hidden_grad, feed_weights
    )

    def core_sum(own, other):
        return (own + core_swap(other).astype(F32)).astype(BF16)

    back_low = core_sum(back_own, back_other)
    back_received = head_swap(back_low)
    done(back_low)
    last_hidden_grad = done(hidden_grads(following(plane_cotangent), head % 2, early_tiles, late_tiles))
    feed_own, feed_other = chip_feed(core_index, following(hidden), w_down)
    done(feed_own)
    upstream = back_low.astype(F32) + following(back_received).astype(F32)
    inverse = lax.rsqrt(jnp.mean(middle * middle, axis=-1, keepdims=True) + 1e-05)
    middle_grad = cotangent.astype(F32) + norm_back(middle, inverse, gain_mlp, upstream)
    branch_low = middle_grad.astype(BF16)
    blocks = joined(spot_index, heads, dot_back(branch_low, w_out).astype(BF16), branch_low)
    done(blocks)
    own_normed = gathered(following(my_half(normed_low)))
    upstream = exchange(blocks)
    feed_low = done(core_sum(following(feed_own), feed_other))
    feed_received = head_swap(feed_low)

    def plane_piece(first, count, hidden_grad):
        kept, given = plane_weight_grads(
            position,
            share,
            following(plane_second),
            plane_cotangent,
            hidden_grad,
            feed_weights,
            first,
            count,
        )
        done(given)
        return kept, core_swap(given)

    def plane_halves(kept, received):
        sums = following(kept) + received.astype(F32)
        sums = share_sum(sums.reshape(6, share, features, -1), 1).reshape(3, 2, features, -1)
        sums = done(sums.astype(BF16))
        return sums, pair_swap(done(my_part(sums, 1 - head % 2, 1)))

    first_piece = plane_piece(0, early_tiles, first_hidden_grad)
    feed = following(feed_low).astype(F32) + feed_received.astype(F32)
    output = done((middle + feed).astype(BF16))
    upstream = following(upstream)
    query_grad, own_grad, other_grad = attention_back(
        position,
        share,
        ring,
        head_rows,
        head_kv,
        upstream,
        query_starts,
        query_places,
        cosines,
        sines,
    )
    done(other_grad)
    all_attended = gathered(following(attended))
    received = core_swap(other_grad)
    if share > 1:
        shape = (heads, share, rows, 2 * HD)
        own_grad = share_sum((own_grad + received.astype(F32)).reshape(shape), 1)[:, 0]
        received = jnp.zeros(own_grad.shape, BF16)
    ring_grads = done(
        grad_blocks(position, ring, following(query_grad), own_grad, received, cosines, sines)
    )
    received = exchange(ring_grads)
    other_normed = head_swap(after(own_normed, ring_grads))
    first_halves = plane_halves(*first_piece)
    last_piece = plane_piece(early_tiles, late_tiles, last_hidden_grad)

    normed_part = done(projected_back(position, ring, following(received), w_query, w_key, w_value))
    normed_received = head_swap(normed_part)
    last_halves = plane_halves(*last_piece)
    own_sum, other_sum = attention_weight_grads(
        position,
        share,
        heads,
        own_normed,
        other_normed,
        following(ring_grads).reshape(heads * rows, -1),
    )
    done(other_sum)
    other_received = core_swap(other_sum)
    if share > 1:
        own_sum = (own_sum + other_received.astype(F32)).reshape(heads, share, features, -1)
        own_sum = share_sum(own_sum, 1)[:, 0]
        other_received = jnp.zeros(own_sum.shape, BF16)
    own_sum = after(own_sum, last_halves[1])
    sum_received = exchange(done((following(own_sum) + other_received.astype(F32)).astype(BF16)))
    out_part = done(dot_rows(following(all_attended), following(upstream)[:, :, HD:].reshape(heads * rows, -1)))
    out_part = out_part.reshape(local_width, share, 2, features)
    out_given = done(my_part(out_part, 1 - core, 2).astype(BF16))
    out_sum = my_part(out_part, core, 2) + core_swap(out_given).astype(F32)
    out_sum = share_sum(out_sum, 1).reshape(local_width, features)
    normed_grad = following(normed_part).astype(F32) + normed_received.astype(F32)
    inverse_attn = lax.rsqrt(jnp.mean(inputs * inputs, axis=-1, keepdims=True) + 1e-05)
    input_grad = (middle_grad + norm_back(inputs, inverse_attn, gain_attn, normed_grad)).astype(BF16)
    done(input_grad)

    gate_sum, up_sum, down_sum, feed_gain = feed_sums(
        position,
        [following(first_halves[0]), last_halves[0]],
        [first_halves[1], last_halves[1]],
        w_gate,
        w_up,
    )
    done(feed_gain)
    query_sum, key_sum, value_sum, attention_gain = attention_sums(
        position,
        ring,
        following(sum_received),
        (w_query, w_key, w_value),
    )

    def gain_sum(terms, gain):
        return jnp.sum(terms, axis=1) / lax.dynamic_slice_in_dim(gain, me * features, features, 0)

    gains = jnp.stack([gain_sum(attention_gain, gain_attn), gain_sum(feed_gain, gain_mlp)])
    gains = gains + head_swap(gains)
    return (
        output,
        input_grad,
        query_sum,
        key_sum,
        value_sum,
        out_sum,
        gate_sum,
        up_sum,
        down_sum,
        gains[0],
        gains[1],
    )


def solution(mesh):
    placed = (
        P("seq", None),
        P(),
        P(None, "head"),
        P(None, "head"),
        P(None, "head"),
        P("head", None),
        P(None, "head"),
        P(None, "head"),
        P("head", None),
        P(),
        P(),
        P("seq", None),
    )
    return jax.shard_map(
        local,
        mesh=mesh,
        in_specs=placed,
        out_specs=(
            P("seq", None),
            P("seq", None),
            P("seq", "head"),
            P("seq", "head"),
            P("seq", "head"),
            P("head", "seq"),
            P("seq", "head"),
            P("seq", "head"),
            P("head", "seq"),
            P("seq"),
            P("seq"),
        ),
        check_vma=False,
    )
```

```python
import functools
import math

import jax
import jax.numpy as jnp
from jax import lax
from jax.experimental import pallas as pl
from jax.experimental.pallas import tpu as pltpu
from jax.sharding import PartitionSpec as P

HD = 128
BIAS_LEN = 4096
BF16 = jnp.bfloat16
F32 = jnp.float32
TILE = 256
KEYS = 1024
VMEM = 60 * 1024 * 1024


def frequencies(head_dim):
    half_dim = head_dim // 2
    return jnp.exp(-jnp.arange(half_dim).astype(F32) * (2.0 / head_dim) * math.log(10000.0))


def turning(places, sign):
    angles = places.astype(F32)[..., None] * frequencies(HD)
    cosine, sine = jnp.cos(angles), sign * jnp.sin(angles)
    return jnp.concatenate([cosine, cosine], -1), jnp.concatenate([-sine, sine], -1)


def normalized(values, gain):
    inverse = lax.rsqrt(jnp.mean(values * values, axis=-1, keepdims=True) + 1e-05)
    return values * inverse * gain, inverse


def norm_back(values, inverse, gain, upstream):
    scaled = values * inverse
    weighted = upstream * gain
    return inverse * (weighted - scaled * jnp.mean(weighted * scaled, axis=-1, keepdims=True))


def dot(one, two):
    return jnp.dot(one, two, preferred_element_type=F32)


def dot_rows(one, two):
    return lax.dot_general(one, two, (((0,), (0,)), ((), ())), preferred_element_type=F32)


def dot_back(one, two):
    return lax.dot_general(one, two, (((1,), (1,)), ((), ())), preferred_element_type=F32)


def gated(normed, hidden_grad, gate_w, up_w):
    gate = dot(normed, gate_w)
    upward = dot(normed, up_w)
    gate_sig = jax.nn.sigmoid(gate)
    silu = gate * gate_sig
    hidden_low = (silu * upward).astype(BF16)
    gate_low = (hidden_grad * upward * (gate_sig + silu * (1.0 - gate_sig))).astype(BF16)
    upward_low = (hidden_grad * silu).astype(BF16)
    return hidden_low, gate_low, upward_low


def call(kernel, scalars, grid, in_specs, out_specs, shapes, scratch, flops=0, moved=0, exps=0):
    return pl.pallas_call(
        kernel,
        grid_spec=pltpu.PrefetchScalarGridSpec(
            num_scalar_prefetch=1,
            grid=grid,
            in_specs=in_specs,
            out_specs=out_specs,
            scratch_shapes=scratch,
        ),
        out_shape=shapes,
        compiler_params=pltpu.CompilerParams(vmem_limit_bytes=VMEM),
        cost_estimate=pl.CostEstimate(flops=flops, bytes_accessed=moved, transcendentals=exps),
    )


def array(shape, kind):
    return jax.ShapeDtypeStruct(tuple(shape), kind)


def whole(shape, **more):
    return pl.BlockSpec(tuple(shape), lambda step, place: (0,) * len(shape), **more)


def half_turn(values, cosine, sine):
    return values * cosine + pltpu.roll(values, HD // 2, 1) * sine


def heads_kernel(place, x, gain, cosine, sine, w_query, w_key, w_value, normed, blocks):
    step = pl.program_id(0)

    @pl.when(step == 0)
    def _():
        values = x[...].astype(F32)
        inverse = lax.rsqrt(jnp.mean(values * values, axis=-1, keepdims=True) + 1e-05)
        normed[...] = (values * inverse * gain[...]).astype(BF16)

    low = normed[...]
    count = w_query.shape[1] // HD
    for index, weight in enumerate((w_query, w_key, w_value)):
        part = dot(low, weight[...])
        for head in range(count):
            values = part[:, head * HD : (head + 1) * HD]
            if index < 2:
                values = half_turn(values, cosine[...], sine[...])
            spot = place[step * count + head]
            blocks[spot, :, index * HD : (index + 1) * HD] = values.astype(BF16)


def head_blocks(spots, x, gain, cosine, sine, w_query, w_key, w_value):
    rows, width = x.shape
    heads = w_query.shape[1] // HD
    weight = pl.BlockSpec((width, 4 * HD), lambda step, place: (0, step))
    blocks = (heads, rows, 3 * HD)
    return call(
        heads_kernel,
        spots,
        (heads // 4,),
        [whole((rows, width)), whole((1, width)), whole((rows, HD)), whole((rows, HD))]
        + [weight] * 3,
        [whole((rows, width)), whole(blocks)],
        [array((rows, width), BF16), array(blocks, BF16)],
        [],
        flops=36 * rows * width * heads * HD,
        moved=6 * width * heads * HD,
    )(spots, x, gain[None], cosine, sine, w_query, w_key, w_value)


def join_kernel(heads, place, mixed_grad, low, blocks):
    columns = low.shape[1] // heads
    for head in range(heads):
        blocks[place[head], :, :HD] = mixed_grad[:, head * HD : (head + 1) * HD]
        blocks[place[head], :, HD:] = low[:, head * columns : (head + 1) * columns]


def joined(spots, heads, mixed_grad, low):
    rows, width = low.shape
    blocks = (heads, rows, HD + width // heads)
    return call(
        functools.partial(join_kernel, heads),
        spots,
        (1,),
        [whole(mixed_grad.shape), whole(low.shape)],
        whole(blocks),
        array(blocks, BF16),
        [],
        moved=40 * rows * width,
    )(spots, mixed_grad, low)


def back_kernel(
    share, ring, place, received, pair, upstream, starts, places, cosine, sine,
    query_grad, own, other, total,
):
    heads, rows = received.shape[:2]
    core = place[2]
    group = 2 * share * rows
    scale = HD ** (-0.5)
    total[...] = jnp.zeros_like(total)
    for block, source in enumerate(ring):
        q, grad = received[block, :, :HD], upstream[block, :, :HD]
        start, spot = starts[block : block + 1], places[block : block + 1]
        sum_query = jnp.zeros((rows, HD), F32)
        for first in range(0, (source + 1) * group, KEYS):
            size = min(KEYS, (source + 1) * group - first)
            keys = pl.ds(first, size)
            k, v = pair[keys, :HD], pair[keys, HD:]
            scores = dot_back(k, q) * scale - math.log(BIAS_LEN)
            key_places = first + lax.broadcasted_iota(jnp.int32, (size, rows), 0)
            allowed = (key_places >= start) & (key_places <= spot)
            weights = jnp.where(allowed, jax.nn.sigmoid(scores), 0.0)
            total[keys, HD:] += dot(weights.astype(BF16), grad)
            score_grad = (dot_back(v, grad) * weights * (1.0 - weights)).astype(BF16)
            total[keys, :HD] += dot(score_grad, q) * scale
            sum_query += dot_rows(score_grad, k)
        query_grad[block] = half_turn(sum_query * scale, cosine[block], sine[block]).astype(BF16)
    both = total[...].reshape(heads * share, 2, rows, 2 * HD)
    mine, theirs = both[:, 0], both[:, 1]
    own[...] = jnp.where(core == 0, mine, theirs)
    other[...] = jnp.where(core == 0, theirs, mine).astype(BF16)


def attention_back(place, share, ring, received, pair, upstream, starts, places, cosine, sine):
    heads, rows = received.shape[:2]
    total = pair.shape[0]
    halves = (heads * share, rows, 2 * HD)
    block = (heads, rows, HD)
    return call(
        functools.partial(back_kernel, share, ring),
        place,
        (1,),
        [whole(received.shape), whole(pair.shape), whole(upstream.shape)]
        + [whole((heads, rows))] * 2
        + [whole(block)] * 2,
        [whole(block), whole(halves), whole(halves)],
        [array(block, BF16), array(halves, F32), array(halves, BF16)],
        [pltpu.VMEM((total, 2 * HD), F32)],
        flops=36 * heads * rows * total * HD,
        moved=8 * total * HD,
        exps=heads * rows * total,
    )(place, received, pair, upstream, starts, places, cosine, sine)


def grads_kernel(ring, place, query_grad, own, received, cosine, sine, blocks):
    for index, source in enumerate(ring):
        both = own[source] + received[source].astype(F32)
        key = half_turn(both[:, :HD], cosine[index], sine[index])
        blocks[index, :, :HD] = query_grad[index]
        blocks[index, :, HD : 2 * HD] = key.astype(BF16)
        blocks[index, :, 2 * HD :] = both[:, HD:].astype(BF16)


def grad_blocks(place, ring, query_grad, own, received, cosine, sine):
    heads, rows = query_grad.shape[:2]
    block = (heads, rows, HD)
    blocks = (heads, rows, 3 * HD)
    return call(
        functools.partial(grads_kernel, ring),
        place,
        (1,),
        [whole(block), whole(own.shape), whole(received.shape), whole(block), whole(block)],
        whole(blocks),
        array(blocks, BF16),
        [],
        moved=90 * heads * rows * HD,
    )(place, query_grad, own, received, cosine, sine)


def project_back_kernel(ring, place, blocks, w_query, w_key, w_value, out, held):
    @pl.when(pl.program_id(0) == 0)
    def _():
        for index, head in enumerate(ring):
            for part in range(3):
                held[part, :, head * HD : (head + 1) * HD] = blocks[
                    index, :, part * HD : (part + 1) * HD
                ]

    out[...] = (
        dot_back(held[0], w_query[...])
        + dot_back(held[1], w_key[...])
        + dot_back(held[2], w_value[...])
    ).astype(BF16)


def projected_back(place, ring, blocks, w_query, w_key, w_value):
    rows = blocks.shape[1]
    width, local_width = w_query.shape
    weight = pl.BlockSpec((4 * TILE, local_width), lambda step, place: (step, 0))
    return call(
        functools.partial(project_back_kernel, ring),
        place,
        (width // (4 * TILE),),
        [whole(blocks.shape)] + [weight] * 3,
        pl.BlockSpec((rows, 4 * TILE), lambda step, place: (0, step)),
        array((rows, width), BF16),
        [pltpu.VMEM((3, rows, local_width), BF16)],
        flops=42 * rows * width * local_width,
        moved=6 * width * local_width,
    )(place, blocks, w_query, w_key, w_value)


def chip_kernel(
    half, own_normed, other_normed, hidden_grad, gate_w, up_w,
    back_own, back_other, hidden, normed, back_sum,
):
    step = pl.program_id(0)
    rows = own_normed.shape[0]

    @pl.when(step == 0)
    def _():
        normed[:rows] = own_normed[...]
        normed[rows:] = other_normed[...]
        back_sum[...] = jnp.zeros_like(back_sum)

    hidden[...], gate_low, upward_low = gated(
        normed[...], hidden_grad[...].astype(F32), gate_w[...], up_w[...]
    )
    back_sum[...] += dot_back(gate_low, gate_w[...]) + dot_back(upward_low, up_w[...])

    @pl.when(step == pl.num_programs(0) - 1)
    def _():
        back_own[...] = back_sum[:rows]
        back_other[...] = back_sum[rows:].astype(BF16)


def feed_kernel(half, hidden, weight, feed_own, feed_other):
    total = dot(hidden[...], weight[...])
    rows = feed_own.shape[0]
    feed_own[...] = total[:rows]
    feed_other[...] = total[rows:].astype(BF16)


def weight_specs(width, first, steps):
    def tile(step, place):
        return place[0] * steps + first + step

    columns = pl.BlockSpec((width, TILE), lambda step, place: (0, tile(step, place)))
    return [columns, columns, pl.BlockSpec((TILE, width), lambda step, place: (tile(step, place), 0))]


def chip_back(half, own_normed, other_normed, hidden_grad, weights):
    rows, width = own_normed.shape
    size = 2 * TILE
    steps = weights[0].shape[1] // 2 // size
    block = whole((rows, width))
    weight = pl.BlockSpec((width, size), lambda step, place: (0, place[0] * steps + step))
    tile = pl.BlockSpec((2 * rows, size), lambda step, place: (0, step))
    return call(
        chip_kernel,
        half,
        (steps,),
        [block] * 2 + [tile] + [weight] * 2,
        [block] * 2 + [tile],
        [
            array((rows, width), F32),
            array((rows, width), BF16),
            array((2 * rows, steps * size), BF16),
        ],
        [pltpu.VMEM((2 * rows, width), BF16), pltpu.VMEM((2 * rows, width), F32)],
        flops=34 * rows * width * steps * size,
        moved=4 * width * steps * size,
        exps=2 * rows * steps * size,
    )(half, own_normed, other_normed, hidden_grad, *weights[:2])


def chip_feed(half, hidden, w_down):
    tokens, units = hidden.shape
    width = w_down.shape[1]
    block = pl.BlockSpec((tokens // 2, 4 * TILE), lambda step, place: (0, step))
    return call(
        feed_kernel,
        half,
        (width // (4 * TILE),),
        [
            whole((tokens, units)),
            pl.BlockSpec((units, 4 * TILE), lambda step, place: (place[0], step)),
        ],
        [block] * 2,
        [array((tokens // 2, width), F32), array((tokens // 2, width), BF16)],
        [],
        flops=6 * tokens * width * units,
        moved=2 * width * units,
    )(half, hidden, w_down)


def plane_kernel(
    share, place, normed, normed_columns, grad_columns, hidden_grad, gate_w, up_w,
    kept, given, normed_turned, grad_turned, hidden, gate, upward,
):
    @pl.when(pl.program_id(0) == 0)
    def _():
        normed_turned[...] = normed_columns[...].T
        grad_turned[...] = grad_columns[...].T

    for first in range(0, normed.shape[0], TILE):
        rows = pl.ds(first, TILE)
        hidden[rows], gate[rows], upward[rows] = gated(
            normed[rows], hidden_grad[rows].astype(F32), gate_w[...], up_w[...]
        )
    core = place[2]
    for index, (left, right) in enumerate(
        ((normed_turned, gate), (normed_turned, upward), (grad_turned, hidden))
    ):
        both = dot(left[...], right[...]).reshape(2 * share, 2, -1, TILE)
        mine, theirs = both[:, 0].reshape(-1, TILE), both[:, 1].reshape(-1, TILE)
        kept[index] = jnp.where(core == 0, mine, theirs).astype(BF16)
        given[index] = jnp.where(core == 0, theirs, mine).astype(BF16)


def plane_weight_grads(place, share, normed, grads, hidden_grad, weights, first, tiles):
    tokens, width = normed.shape
    steps = weights[0].shape[1] // 2 // TILE
    columns = width // 4
    out = pl.BlockSpec((3, columns // 2, TILE), lambda step, place: (0, 0, step))
    held = pl.BlockSpec((tokens, columns), lambda step, place: (0, place[1]))
    return call(
        functools.partial(plane_kernel, share),
        place,
        (tiles,),
        [
            whole((tokens, width), pipeline_mode=pl.Buffered(1)),
            held,
            held,
            pl.BlockSpec((tokens, TILE), lambda step, place: (0, step)),
        ]
        + weight_specs(width, first, steps)[:2],
        [out, out],
        [array((3, columns // 2, tiles * TILE), BF16)] * 2,
        [pltpu.VMEM((columns, tokens), BF16)] * 2 + [pltpu.VMEM((tokens, TILE), BF16)] * 3,
        flops=4 * tokens * (2 * width + 3 * columns) * tiles * TILE,
        moved=4 * width * tiles * TILE,
        exps=tokens * tiles * TILE,
    )(place, normed, normed, grads, hidden_grad, *weights[:2])


def turn(out, mine, own, *others):
    @pl.when(mine)
    def _():
        out[...] = own[...].T

    @pl.when(jnp.logical_not(mine))
    def _():
        first = 0
        for other in others:
            out[:, first : first + other.shape[0]] = other[...].T
            first += other.shape[0]


def attention_weight_kernel(share, spots, place, own, other, grads, kept, given, turned):
    step = pl.program_id(0)
    turn(turned, step // (pl.num_programs(0) // 2) == place[4], own, other)
    both = dot(turned[...], grads[...]).reshape(2, share, 2, -1, grads.shape[1])
    for index in range(2):
        spot = place[spots + 2 * step + index]
        first = both[index, :, 0].reshape(kept.shape[1:])
        last = both[index, :, 1].reshape(kept.shape[1:])
        kept[spot] = jnp.where(place[2] == 0, first, last)
        given[spot] = jnp.where(place[2] == 0, last, first).astype(BF16)


def attention_weight_grads(place, share, heads, own, other, grads):
    tokens, half_width = own.shape
    tile, count = 4 * half_width // heads, heads // 4
    out = (heads, tile // 4, grads.shape[1])
    columns = pl.BlockSpec((tokens, tile), lambda step, place: (0, step % count))
    return call(
        functools.partial(attention_weight_kernel, share, place.shape[0] - heads),
        place,
        (heads // 2,),
        [columns, columns, whole(grads.shape)],
        [whole(out)] * 2,
        [array(out, F32), array(out, BF16)],
        [pltpu.VMEM((tile, tokens), BF16)],
        flops=12 * tokens * half_width * grads.shape[1],
        moved=8 * tokens * half_width,
    )(place, own, other, grads)


def attention_sums_kernel(ring, place, blocks, *refs):
    weights, sums, gain = refs[:3], refs[3:6], refs[6]
    total = jnp.zeros(gain.shape, F32)
    for index, head in enumerate(ring):
        columns = slice(head * HD, (head + 1) * HD)
        for part in range(3):
            grad = blocks[index, :, part * HD : (part + 1) * HD].astype(F32)
            sums[part][:, columns] = grad
            total += grad * weights[part][:, columns].astype(F32)
    gain[...] = total


def attention_sums(place, ring, blocks, weights):
    rows = blocks.shape[1]
    local_width = weights[0].shape[1]
    out = (rows, local_width)
    return call(
        functools.partial(attention_sums_kernel, ring),
        place,
        (1,),
        [whole(blocks.shape)] + [pl.BlockSpec(out, lambda step, place: (place[3], 0))] * 3,
        [whole(out)] * 3 + [whole((rows, HD))],
        [array(out, F32)] * 3 + [array((rows, HD), F32)],
        [],
        moved=90 * rows * local_width,
    )(place, blocks, *weights)


def feed_sums_kernel(count, place, *refs):
    pieces = refs[:count], refs[count : 2 * count]
    gate_w, up_w, gate_sum, up_sum, down_sum, gain = refs[2 * count :]
    step = pl.program_id(0)

    @pl.when(step == 0)
    def _():
        gain[...] = jnp.zeros_like(gain)

    for source in range(2):

        @pl.when(step == source)
        def _(source=source):
            total = gain[...]
            first = 0
            for piece in pieces[source]:
                columns = slice(first, first + piece.shape[-1])
                first = columns.stop
                gate, up = piece[0].astype(F32), piece[1].astype(F32)
                gate_sum[:, columns] = gate
                up_sum[:, columns] = up
                down_sum[columns] = piece[2].astype(F32).T
                terms = gate * gate_w[:, columns].astype(F32) + up * up_w[:, columns].astype(F32)
                for spot in range(0, terms.shape[1], HD):
                    total += terms[:, spot : spot + HD]
            gain[...] = total


def feed_sums(place, sums, others, w_gate, w_up):
    rows = others[0].shape[1]
    hidden = w_gate.shape[1]

    def half(step, place):
        return place[0] ^ step

    def mine(piece):
        shape = (3, None, rows, piece.shape[-1])
        return pl.BlockSpec(shape, lambda step, place: (0, place[0], 0, 0))

    weight = pl.BlockSpec((rows, hidden // 2), lambda step, place: (place[3], half(step, place)))
    wide = pl.BlockSpec((rows, hidden // 2), lambda step, place: (0, half(step, place)))
    tall = pl.BlockSpec((hidden // 2, rows), lambda step, place: (half(step, place), 0))
    return call(
        functools.partial(feed_sums_kernel, len(sums)),
        place,
        (2,),
        [mine(piece) for piece in sums] + [whole(piece.shape) for piece in others] + [weight] * 2,
        [wide, wide, tall, whole((rows, HD))],
        [
            array((rows, hidden), F32),
            array((rows, hidden), F32),
            array((hidden, rows), F32),
            array((rows, HD), F32),
        ],
        [],
        moved=45 * rows * hidden,
    )(place, *sums, *others, w_gate, w_up)


def local(
    activations,
    doc_ids,
    w_query,
    w_key,
    w_value,
    w_out,
    w_gate,
    w_up,
    w_down,
    gain_attn,
    gain_mlp,
    cotangent,
):
    rows, width = activations.shape
    devices = lax.axis_size("seq")
    total = rows * devices
    features = width // devices
    local_width = w_query.shape[1]
    heads = local_width // HD
    share = devices // (2 * heads)
    me = lax.axis_index("seq")
    core = me % 2
    residue = (me // 2) % share
    head = me // (2 * share)
    tiles = w_gate.shape[1] // 2 // TILE
    feed_weights = (w_gate, w_up, w_down)

    def place(a, r, c):
        return (a * share + r) * 2 + c

    def split(s):
        return s // (2 * share), (s // 2) % share, s % 2

    def permuted(x, target):
        return lax.ppermute(x, "seq", [(s, target(*split(s))) for s in range(devices)])

    def core_swap(x):
        return permuted(x, lambda a, r, c: place(a, r, 1 - c))

    def pair_swap(x):
        return permuted(x, lambda a, r, c: place(a ^ 1, r, c))

    ring = (*range(0, heads, 2), *range(heads - 1, 0, -2))
    spots = [ring.index(a) for a in range(heads)]
    ring_groups = [[place(a, r, c) for a in ring] for r in range(share) for c in range(2)]

    def gathered(x):
        return lax.all_gather(x, "seq", axis=0, tiled=True, axis_index_groups=ring_groups)

    def head_swap(x):
        return lax.ppermute(x, "head", [(0, 1), (1, 0)])

    share_groups = [
        [place(a, r, c) for r in range(share)] for a in range(heads) for c in range(2)
    ]

    def after(x, *earlier):
        return lax.optimization_barrier((x, *earlier))[0]

    def exchange(x):
        return lax.all_to_all(x, "seq", 0, 0, tiled=True, axis_index_groups=ring_groups)

    def by_head(x):
        return jnp.stack([x[spot] for spot in spots])

    def share_sum(x, dim):
        if share == 1:
            return x
        return lax.psum_scatter(
            x, "seq", scatter_dimension=dim, tiled=True, axis_index_groups=share_groups
        )

    def in_core_order(mine, other, axis):
        return jnp.where(core == 0, jnp.stack([mine, other], axis), jnp.stack([other, mine], axis))

    def my_part(x, index, axis):
        return lax.dynamic_index_in_dim(x, index, axis, keepdims=False)

    column = lax.axis_index("head")

    def my_half(x):
        return lax.dynamic_slice_in_dim(x, column * (width // 2), width // 2, 1)

    last = []

    def following(x):
        return after(x, *last)

    def done(x):
        last[:] = [x]
        return x

    my_places = me * rows + jnp.arange(rows, dtype=jnp.int32)
    block_starts = place(jnp.array(ring, jnp.int32), residue, core) * rows
    query_places = block_starts[:, None] + jnp.arange(rows, dtype=jnp.int32)[None, :]
    query_docs = doc_ids.reshape(heads, share, 2, rows)[jnp.array(ring), residue, core]
    query_starts = jnp.sum((doc_ids < query_docs[..., None]).astype(jnp.int32), -1)
    key_places = jnp.arange(total, dtype=jnp.int32)
    allowed = (key_places >= query_starts.reshape(-1, 1)) & (
        key_places <= query_places.reshape(-1, 1)
    )
    scale = HD ** (-0.5)
    core_index = core[None].astype(jnp.int32)
    spot_index = jnp.array(spots, jnp.int32)
    position = jnp.concatenate([jnp.stack([head % 2, head // 2, core, me, column]), spot_index]).astype(jnp.int32)

    plane_cotangent = gathered(cotangent)
    inputs = activations.astype(F32)
    cosine, sine = turning(my_places, 1.0)
    normed_low, blocks = head_blocks(
        spot_index, activations, gain_attn, cosine, sine, w_query, w_key, w_value
    )
    chip_cotangent = jnp.concatenate([cotangent, core_swap(cotangent)], 0)
    early_tiles = tiles * 4 // 8
    late_tiles = tiles - early_tiles
    def hidden_grads(grads, half, first, count):
        start = (half * tiles + first) * TILE
        return dot_back(grads, lax.dynamic_slice_in_dim(w_down, start, count * TILE, 0)).astype(BF16)

    chip_grads = after(chip_cotangent, blocks)
    chip_hidden_grad = hidden_grads(chip_grads, core, 0, tiles)
    head_rows = after(exchange(blocks), chip_hidden_grad)

    def all_keys(own):
        if share > 1:
            own = lax.all_gather(own, "seq", axis=1, axis_index_groups=share_groups)
        else:
            own = own[:, None]
        return in_core_order(own, core_swap(own), 2).reshape(total, 2 * HD)

    head_kv = all_keys(by_head(head_rows[:, :, HD:]))
    scores = dot_back(head_rows[:, :, :HD].reshape(heads * rows, HD), head_kv[:, :HD])
    weights = jnp.where(allowed, jax.nn.sigmoid(scores * scale - math.log(BIAS_LEN)), 0.0)
    head_mixed = dot(weights.astype(BF16), head_kv[:, HD:]).astype(BF16)
    attended = by_head(exchange(head_mixed.reshape(heads, rows, HD)))
    attended = attended.transpose(1, 0, 2).reshape(rows, -1)

    branch = dot(attended, w_out).astype(BF16)
    branch_received = head_swap(branch)
    cosines, sines = turning(after(query_places, branch), -1.0)
    first_hidden_grad = hidden_grads(
        after(plane_cotangent, branch, cosines, sines), head % 2, 0, early_tiles
    )
    branch_received = after(branch_received, first_hidden_grad)
    middle = inputs + (branch.astype(F32) + branch_received.astype(F32))
    second, _ = normalized(middle, gain_mlp)
    second_low = second.astype(BF16)
    plane_second = gathered(second_low)

    back_own, back_other, hidden = chip_back(
        core_index, second_low, core_swap(second_low), chip_hidden_grad, feed_weights
    )

    def core_sum(own, other):
        return (own + core_swap(other).astype(F32)).astype(BF16)

    back_low = core_sum(back_own, back_other)
    back_received = head_swap(back_low)
    done(back_low)
    last_hidden_grad = done(hidden_grads(following(plane_cotangent), head % 2, early_tiles, late_tiles))
    feed_own, feed_other = chip_feed(core_index, following(hidden), w_down)
    done(feed_own)
    upstream = back_low.astype(F32) + following(back_received).astype(F32)
    inverse = lax.rsqrt(jnp.mean(middle * middle, axis=-1, keepdims=True) + 1e-05)
    middle_grad = cotangent.astype(F32) + norm_back(middle, inverse, gain_mlp, upstream)
    branch_low = middle_grad.astype(BF16)
    blocks = joined(spot_index, heads, dot_back(branch_low, w_out).astype(BF16), branch_low)
    done(blocks)
    own_normed = gathered(following(my_half(normed_low)))
    upstream = exchange(blocks)
    feed_low = done(core_sum(following(feed_own), feed_other))
    feed_received = head_swap(feed_low)

    def plane_piece(first, count, hidden_grad):
        kept, given = plane_weight_grads(
            position,
            share,
            following(plane_second),
            plane_cotangent,
            hidden_grad,
            feed_weights,
            first,
            count,
        )
        done(given)
        return kept, core_swap(given)

    def plane_halves(kept, received):
        sums = following(kept).astype(F32) + received.astype(F32)
        sums = share_sum(sums.reshape(6, share, features, -1), 1).reshape(3, 2, features, -1)
        sums = done(sums.astype(BF16))
        return sums, pair_swap(done(my_part(sums, 1 - head % 2, 1)))

    first_piece = plane_piece(0, early_tiles, first_hidden_grad)
    feed = following(feed_low).astype(F32) + feed_received.astype(F32)
    output = done((middle + feed).astype(BF16))
    upstream = following(upstream)
    query_grad, own_grad, other_grad = attention_back(
        position,
        share,
        ring,
        head_rows,
        head_kv,
        upstream,
        query_starts,
        query_places,
        cosines,
        sines,
    )
    done(other_grad)
    all_attended = gathered(following(attended))
    received = core_swap(other_grad)
    if share > 1:
        shape = (heads, share, rows, 2 * HD)
        own_grad = share_sum((own_grad + received.astype(F32)).reshape(shape), 1)[:, 0]
        received = jnp.zeros(own_grad.shape, BF16)
    ring_grads = done(
        grad_blocks(position, ring, following(query_grad), own_grad, received, cosines, sines)
    )
    received = exchange(ring_grads)
    other_normed = head_swap(after(own_normed, ring_grads))
    first_halves = plane_halves(*first_piece)
    last_piece = plane_piece(early_tiles, late_tiles, last_hidden_grad)

    normed_part = done(projected_back(position, ring, following(received), w_query, w_key, w_value))
    normed_received = head_swap(normed_part)
    last_halves = plane_halves(*last_piece)
    own_sum, other_sum = attention_weight_grads(
        position,
        share,
        heads,
        own_normed,
        other_normed,
        following(ring_grads).reshape(heads * rows, -1),
    )
    done(other_sum)
    other_received = core_swap(other_sum)
    if share > 1:
        own_sum = (own_sum + other_received.astype(F32)).reshape(heads, share, features, -1)
        own_sum = share_sum(own_sum, 1)[:, 0]
        other_received = jnp.zeros(own_sum.shape, BF16)
    own_sum = after(own_sum, last_halves[1])
    sum_received = exchange(done((following(own_sum) + other_received.astype(F32)).astype(BF16)))
    out_part = done(dot_rows(following(all_attended), following(upstream)[:, :, HD:].reshape(heads * rows, -1)))
    out_part = out_part.reshape(local_width, share, 2, features)
    out_given = done(my_part(out_part, 1 - core, 2).astype(BF16))
    out_sum = my_part(out_part, core, 2) + core_swap(out_given).astype(F32)
    out_sum = share_sum(out_sum, 1).reshape(local_width, features)
    normed_grad = following(normed_part).astype(F32) + normed_received.astype(F32)
    inverse_attn = lax.rsqrt(jnp.mean(inputs * inputs, axis=-1, keepdims=True) + 1e-05)
    input_grad = (middle_grad + norm_back(inputs, inverse_attn, gain_attn, normed_grad)).astype(BF16)
    done(input_grad)

    gate_sum, up_sum, down_sum, feed_gain = feed_sums(
        position,
        [following(first_halves[0]), last_halves[0]],
        [first_halves[1], last_halves[1]],
        w_gate,
        w_up,
    )
    done(feed_gain)
    query_sum, key_sum, value_sum, attention_gain = attention_sums(
        position,
        ring,
        following(sum_received),
        (w_query, w_key, w_value),
    )

    def gain_sum(terms, gain):
        return jnp.sum(terms, axis=1) / lax.dynamic_slice_in_dim(gain, me * features, features, 0)

    gains = jnp.stack([gain_sum(attention_gain, gain_attn), gain_sum(feed_gain, gain_mlp)])
    gains = gains + head_swap(gains)
    return (
        output,
        input_grad,
        query_sum,
        key_sum,
        value_sum,
        out_sum,
        gate_sum,
        up_sum,
        down_sum,
        gains[0],
        gains[1],
    )


def solution(mesh):
    placed = (
        P("seq", None),
        P(),
        P(None, "head"),
        P(None, "head"),
        P(None, "head"),
        P("head", None),
        P(None, "head"),
        P(None, "head"),
        P("head", None),
        P(),
        P(),
        P("seq", None),
    )
    return jax.shard_map(
        local,
        mesh=mesh,
        in_specs=placed,
        out_specs=(
            P("seq", None),
            P("seq", None),
            P("seq", "head"),
            P("seq", "head"),
            P("seq", "head"),
            P("head", "seq"),
            P("seq", "head"),
            P("seq", "head"),
            P("head", "seq"),
            P("seq"),
            P("seq"),
        ),
        check_vma=False,
    )
```

```python
import functools
import math

import jax
import jax.numpy as jnp
from jax import lax
from jax.experimental import pallas as pl
from jax.experimental.pallas import tpu as pltpu
from jax.sharding import PartitionSpec as P

HD = 128
BIAS_LEN = 4096
BF16 = jnp.bfloat16
F32 = jnp.float32
TILE = 256
KEYS = 1024
VMEM = 60 * 1024 * 1024


def frequencies(head_dim):
    half_dim = head_dim // 2
    return jnp.exp(-jnp.arange(half_dim).astype(F32) * (2.0 / head_dim) * math.log(10000.0))


def turning(places, sign):
    angles = places.astype(F32)[..., None] * frequencies(HD)
    cosine, sine = jnp.cos(angles), sign * jnp.sin(angles)
    return jnp.concatenate([cosine, cosine], -1), jnp.concatenate([-sine, sine], -1)


def normalized(values, gain):
    inverse = lax.rsqrt(jnp.mean(values * values, axis=-1, keepdims=True) + 1e-05)
    return values * inverse * gain, inverse


def norm_back(values, inverse, gain, upstream):
    scaled = values * inverse
    weighted = upstream * gain
    return inverse * (weighted - scaled * jnp.mean(weighted * scaled, axis=-1, keepdims=True))


def dot(one, two):
    return jnp.dot(one, two, preferred_element_type=F32)


def dot_rows(one, two):
    return lax.dot_general(one, two, (((0,), (0,)), ((), ())), preferred_element_type=F32)


def dot_back(one, two):
    return lax.dot_general(one, two, (((1,), (1,)), ((), ())), preferred_element_type=F32)


def gated(normed, hidden_grad, gate_w, up_w):
    gate = dot(normed, gate_w)
    upward = dot(normed, up_w)
    gate_sig = jax.nn.sigmoid(gate)
    silu = gate * gate_sig
    hidden_low = (silu * upward).astype(BF16)
    gate_low = (hidden_grad * upward * (gate_sig + silu * (1.0 - gate_sig))).astype(BF16)
    upward_low = (hidden_grad * silu).astype(BF16)
    return hidden_low, gate_low, upward_low


def call(kernel, scalars, grid, in_specs, out_specs, shapes, scratch, flops=0, moved=0, exps=0):
    return pl.pallas_call(
        kernel,
        grid_spec=pltpu.PrefetchScalarGridSpec(
            num_scalar_prefetch=1,
            grid=grid,
            in_specs=in_specs,
            out_specs=out_specs,
            scratch_shapes=scratch,
        ),
        out_shape=shapes,
        compiler_params=pltpu.CompilerParams(vmem_limit_bytes=VMEM),
        cost_estimate=pl.CostEstimate(flops=flops, bytes_accessed=moved, transcendentals=exps),
    )


def array(shape, kind):
    return jax.ShapeDtypeStruct(tuple(shape), kind)


def whole(shape, **more):
    return pl.BlockSpec(tuple(shape), lambda step, place: (0,) * len(shape), **more)


def half_turn(values, cosine, sine):
    return values * cosine + pltpu.roll(values, HD // 2, 1) * sine


def heads_kernel(place, x, gain, cosine, sine, w_query, w_key, w_value, normed, blocks):
    step = pl.program_id(0)

    @pl.when(step == 0)
    def _():
        values = x[...].astype(F32)
        inverse = lax.rsqrt(jnp.mean(values * values, axis=-1, keepdims=True) + 1e-05)
        normed[...] = (values * inverse * gain[...]).astype(BF16)

    low = normed[...]
    count = w_query.shape[1] // HD
    for index, weight in enumerate((w_query, w_key, w_value)):
        part = dot(low, weight[...])
        for head in range(count):
            values = part[:, head * HD : (head + 1) * HD]
            if index < 2:
                values = half_turn(values, cosine[...], sine[...])
            spot = place[step * count + head]
            blocks[spot, :, index * HD : (index + 1) * HD] = values.astype(BF16)


def head_blocks(spots, x, gain, cosine, sine, w_query, w_key, w_value):
    rows, width = x.shape
    heads = w_query.shape[1] // HD
    weight = pl.BlockSpec((width, 4 * HD), lambda step, place: (0, step))
    blocks = (heads, rows, 3 * HD)
    return call(
        heads_kernel,
        spots,
        (heads // 4,),
        [whole((rows, width)), whole((1, width)), whole((rows, HD)), whole((rows, HD))]
        + [weight] * 3,
        [whole((rows, width)), whole(blocks)],
        [array((rows, width), BF16), array(blocks, BF16)],
        [],
        flops=36 * rows * width * heads * HD,
        moved=6 * width * heads * HD,
    )(spots, x, gain[None], cosine, sine, w_query, w_key, w_value)


def join_kernel(heads, place, mixed_grad, low, blocks):
    columns = low.shape[1] // heads
    for head in range(heads):
        blocks[place[head], :, :HD] = mixed_grad[:, head * HD : (head + 1) * HD]
        blocks[place[head], :, HD:] = low[:, head * columns : (head + 1) * columns]


def joined(spots, heads, mixed_grad, low):
    rows, width = low.shape
    blocks = (heads, rows, HD + width // heads)
    return call(
        functools.partial(join_kernel, heads),
        spots,
        (1,),
        [whole(mixed_grad.shape), whole(low.shape)],
        whole(blocks),
        array(blocks, BF16),
        [],
        moved=40 * rows * width,
    )(spots, mixed_grad, low)


def back_kernel(
    share, ring, place, received, pair, upstream, starts, places, cosine, sine,
    query_grad, own, other, total,
):
    heads, rows = received.shape[:2]
    core = place[2]
    group = 2 * share * rows
    scale = HD ** (-0.5)
    total[...] = jnp.zeros_like(total)
    for block, source in enumerate(ring):
        q, grad = received[block, :, :HD], upstream[block, :, :HD]
        start, spot = starts[block : block + 1], places[block : block + 1]
        sum_query = jnp.zeros((rows, HD), F32)
        for first in range(0, (source + 1) * group, KEYS):
            size = min(KEYS, (source + 1) * group - first)
            keys = pl.ds(first, size)
            k, v = pair[keys, :HD], pair[keys, HD:]
            scores = dot_back(k, q) * scale - math.log(BIAS_LEN)
            key_places = first + lax.broadcasted_iota(jnp.int32, (size, rows), 0)
            allowed = (key_places >= start) & (key_places <= spot)
            weights = jnp.where(allowed, jax.nn.sigmoid(scores), 0.0)
            total[keys, HD:] += dot(weights.astype(BF16), grad)
            score_grad = (dot_back(v, grad) * weights * (1.0 - weights)).astype(BF16)
            total[keys, :HD] += dot(score_grad, q) * scale
            sum_query += dot_rows(score_grad, k)
        query_grad[block] = half_turn(sum_query * scale, cosine[block], sine[block]).astype(BF16)
    both = total[...].reshape(heads * share, 2, rows, 2 * HD)
    mine, theirs = both[:, 0], both[:, 1]
    own[...] = jnp.where(core == 0, mine, theirs)
    other[...] = jnp.where(core == 0, theirs, mine).astype(BF16)


def attention_back(place, share, ring, received, pair, upstream, starts, places, cosine, sine):
    heads, rows = received.shape[:2]
    total = pair.shape[0]
    halves = (heads * share, rows, 2 * HD)
    block = (heads, rows, HD)
    return call(
        functools.partial(back_kernel, share, ring),
        place,
        (1,),
        [whole(received.shape), whole(pair.shape), whole(upstream.shape)]
        + [whole((heads, rows))] * 2
        + [whole(block)] * 2,
        [whole(block), whole(halves), whole(halves)],
        [array(block, BF16), array(halves, F32), array(halves, BF16)],
        [pltpu.VMEM((total, 2 * HD), F32)],
        flops=36 * heads * rows * total * HD,
        moved=8 * total * HD,
        exps=heads * rows * total,
    )(place, received, pair, upstream, starts, places, cosine, sine)


def grads_kernel(ring, place, query_grad, own, received, cosine, sine, blocks):
    for index, source in enumerate(ring):
        both = own[source] + received[source].astype(F32)
        key = half_turn(both[:, :HD], cosine[index], sine[index])
        blocks[index, :, :HD] = query_grad[index]
        blocks[index, :, HD : 2 * HD] = key.astype(BF16)
        blocks[index, :, 2 * HD :] = both[:, HD:].astype(BF16)


def grad_blocks(place, ring, query_grad, own, received, cosine, sine):
    heads, rows = query_grad.shape[:2]
    block = (heads, rows, HD)
    blocks = (heads, rows, 3 * HD)
    return call(
        functools.partial(grads_kernel, ring),
        place,
        (1,),
        [whole(block), whole(own.shape), whole(received.shape), whole(block), whole(block)],
        whole(blocks),
        array(blocks, BF16),
        [],
        moved=90 * heads * rows * HD,
    )(place, query_grad, own, received, cosine, sine)


def project_back_kernel(ring, place, blocks, w_query, w_key, w_value, out, held):
    @pl.when(pl.program_id(0) == 0)
    def _():
        for index, head in enumerate(ring):
            for part in range(3):
                held[part, :, head * HD : (head + 1) * HD] = blocks[
                    index, :, part * HD : (part + 1) * HD
                ]

    out[...] = (
        dot_back(held[0], w_query[...])
        + dot_back(held[1], w_key[...])
        + dot_back(held[2], w_value[...])
    ).astype(BF16)


def projected_back(place, ring, blocks, w_query, w_key, w_value):
    rows = blocks.shape[1]
    width, local_width = w_query.shape
    weight = pl.BlockSpec((4 * TILE, local_width), lambda step, place: (step, 0))
    return call(
        functools.partial(project_back_kernel, ring),
        place,
        (width // (4 * TILE),),
        [whole(blocks.shape)] + [weight] * 3,
        pl.BlockSpec((rows, 4 * TILE), lambda step, place: (0, step)),
        array((rows, width), BF16),
        [pltpu.VMEM((3, rows, local_width), BF16)],
        flops=42 * rows * width * local_width,
        moved=6 * width * local_width,
    )(place, blocks, w_query, w_key, w_value)


def chip_kernel(
    half, own_normed, other_normed, hidden_grad, gate_w, up_w,
    back_own, back_other, hidden, normed, back_sum,
):
    step = pl.program_id(0)
    rows = own_normed.shape[0]

    @pl.when(step == 0)
    def _():
        normed[:rows] = own_normed[...]
        normed[rows:] = other_normed[...]
        back_sum[...] = jnp.zeros_like(back_sum)

    hidden[...], gate_low, upward_low = gated(
        normed[...], hidden_grad[...].astype(F32), gate_w[...], up_w[...]
    )
    back_sum[...] += dot_back(gate_low, gate_w[...]) + dot_back(upward_low, up_w[...])

    @pl.when(step == pl.num_programs(0) - 1)
    def _():
        back_own[...] = back_sum[:rows]
        back_other[...] = back_sum[rows:].astype(BF16)


def feed_kernel(half, hidden, weight, feed_own, feed_other):
    total = dot(hidden[...], weight[...])
    rows = feed_own.shape[0]
    feed_own[...] = total[:rows]
    feed_other[...] = total[rows:].astype(BF16)


def weight_specs(width, first, steps):
    def tile(step, place):
        return place[0] * steps + first + step

    columns = pl.BlockSpec((width, TILE), lambda step, place: (0, tile(step, place)))
    return [columns, columns, pl.BlockSpec((TILE, width), lambda step, place: (tile(step, place), 0))]


def chip_back(half, own_normed, other_normed, hidden_grad, weights):
    rows, width = own_normed.shape
    size = 2 * TILE
    steps = weights[0].shape[1] // 2 // size
    block = whole((rows, width))
    weight = pl.BlockSpec((width, size), lambda step, place: (0, place[0] * steps + step))
    tile = pl.BlockSpec((2 * rows, size), lambda step, place: (0, step))
    return call(
        chip_kernel,
        half,
        (steps,),
        [block] * 2 + [tile] + [weight] * 2,
        [block] * 2 + [tile],
        [
            array((rows, width), F32),
            array((rows, width), BF16),
            array((2 * rows, steps * size), BF16),
        ],
        [pltpu.VMEM((2 * rows, width), BF16), pltpu.VMEM((2 * rows, width), F32)],
        flops=34 * rows * width * steps * size,
        moved=4 * width * steps * size,
        exps=2 * rows * steps * size,
    )(half, own_normed, other_normed, hidden_grad, *weights[:2])


def chip_feed(half, hidden, w_down):
    tokens, units = hidden.shape
    width = w_down.shape[1]
    block = pl.BlockSpec((tokens // 2, 4 * TILE), lambda step, place: (0, step))
    return call(
        feed_kernel,
        half,
        (width // (4 * TILE),),
        [
            whole((tokens, units)),
            pl.BlockSpec((units, 4 * TILE), lambda step, place: (place[0], step)),
        ],
        [block] * 2,
        [array((tokens // 2, width), F32), array((tokens // 2, width), BF16)],
        [],
        flops=6 * tokens * width * units,
        moved=2 * width * units,
    )(half, hidden, w_down)


def plane_kernel(
    share, place, normed, normed_columns, grad_columns, hidden_grad, gate_w, up_w,
    kept, given, normed_turned, grad_turned, hidden, gate, upward,
):
    @pl.when(pl.program_id(0) == 0)
    def _():
        normed_turned[...] = normed_columns[...].T
        grad_turned[...] = grad_columns[...].T

    for first in range(0, normed.shape[0], TILE):
        rows = pl.ds(first, TILE)
        hidden[rows], gate[rows], upward[rows] = gated(
            normed[rows], hidden_grad[rows].astype(F32), gate_w[...], up_w[...]
        )
    core = place[2]
    for index, (left, right) in enumerate(
        ((normed_turned, gate), (normed_turned, upward), (grad_turned, hidden))
    ):
        both = dot(left[...], right[...]).reshape(2 * share, 2, -1, TILE)
        mine, theirs = both[:, 0].reshape(-1, TILE), both[:, 1].reshape(-1, TILE)
        kept[index] = jnp.where(core == 0, mine, theirs).astype(BF16)
        given[index] = jnp.where(core == 0, theirs, mine).astype(BF16)


def plane_weight_grads(place, share, normed, grads, hidden_grad, weights, first, tiles):
    tokens, width = normed.shape
    steps = weights[0].shape[1] // 2 // TILE
    columns = width // 4
    out = pl.BlockSpec((3, columns // 2, TILE), lambda step, place: (0, 0, step))
    held = pl.BlockSpec((tokens, columns), lambda step, place: (0, place[1]))
    return call(
        functools.partial(plane_kernel, share),
        place,
        (tiles,),
        [
            whole((tokens, width), pipeline_mode=pl.Buffered(1)),
            held,
            held,
            pl.BlockSpec((tokens, TILE), lambda step, place: (0, step)),
        ]
        + weight_specs(width, first, steps)[:2],
        [out, out],
        [array((3, columns // 2, tiles * TILE), BF16)] * 2,
        [pltpu.VMEM((columns, tokens), BF16)] * 2 + [pltpu.VMEM((tokens, TILE), BF16)] * 3,
        flops=4 * tokens * (2 * width + 3 * columns) * tiles * TILE,
        moved=4 * width * tiles * TILE,
        exps=tokens * tiles * TILE,
    )(place, normed, normed, grads, hidden_grad, *weights[:2])


def turn(out, mine, own, *others):
    @pl.when(mine)
    def _():
        out[...] = own[...].T

    @pl.when(jnp.logical_not(mine))
    def _():
        first = 0
        for other in others:
            out[:, first : first + other.shape[0]] = other[...].T
            first += other.shape[0]


def attention_weight_kernel(share, spots, place, own, other, grads, kept, given, turned):
    step = pl.program_id(0)
    turn(turned, step // (pl.num_programs(0) // 2) == place[4], own, other)
    both = dot(turned[...], grads[...]).reshape(2, share, 2, -1, grads.shape[1])
    for index in range(2):
        spot = place[spots + 2 * step + index]
        first = both[index, :, 0].reshape(kept.shape[1:])
        last = both[index, :, 1].reshape(kept.shape[1:])
        kept[spot] = jnp.where(place[2] == 0, first, last).astype(BF16)
        given[spot] = jnp.where(place[2] == 0, last, first).astype(BF16)


def attention_weight_grads(place, share, heads, own, other, grads):
    tokens, half_width = own.shape
    tile, count = 4 * half_width // heads, heads // 4
    out = (heads, tile // 4, grads.shape[1])
    columns = pl.BlockSpec((tokens, tile), lambda step, place: (0, step % count))
    return call(
        functools.partial(attention_weight_kernel, share, place.shape[0] - heads),
        place,
        (heads // 2,),
        [columns, columns, whole(grads.shape)],
        [whole(out)] * 2,
        [array(out, BF16)] * 2,
        [pltpu.VMEM((tile, tokens), BF16)],
        flops=12 * tokens * half_width * grads.shape[1],
        moved=8 * tokens * half_width,
    )(place, own, other, grads)


def attention_sums_kernel(ring, place, blocks, *refs):
    weights, sums, gain = refs[:3], refs[3:6], refs[6]
    total = jnp.zeros((blocks.shape[1], HD), F32)
    for index, head in enumerate(ring):
        columns = slice(head * HD, (head + 1) * HD)
        for part in range(3):
            grad = blocks[index, :, part * HD : (part + 1) * HD].astype(F32)
            sums[part][:, columns] = grad
            total += grad * weights[part][:, columns].astype(F32)
    gain[...] = jnp.sum(total.T, axis=0, keepdims=True)


def attention_sums(place, ring, blocks, weights):
    rows = blocks.shape[1]
    local_width = weights[0].shape[1]
    out = (rows, local_width)
    return call(
        functools.partial(attention_sums_kernel, ring),
        place,
        (1,),
        [whole(blocks.shape)] + [pl.BlockSpec(out, lambda step, place: (place[3], 0))] * 3,
        [whole(out)] * 3 + [whole((1, rows))],
        [array(out, F32)] * 3 + [array((1, rows), F32)],
        [],
        moved=90 * rows * local_width,
    )(place, blocks, *weights)


def feed_sums_kernel(count, place, *refs):
    pieces = refs[:count], refs[count : 2 * count]
    gate_w, up_w, gate_sum, up_sum, down_sum, gain = refs[2 * count :]
    step = pl.program_id(0)

    @pl.when(step == 0)
    def _():
        gain[...] = jnp.zeros_like(gain)

    for source in range(2):

        @pl.when(step == source)
        def _(source=source):
            total = gain[...]
            first = 0
            for piece in pieces[source]:
                columns = slice(first, first + piece.shape[-1])
                first = columns.stop
                gate, up = piece[0].astype(F32), piece[1].astype(F32)
                gate_sum[:, columns] = gate
                up_sum[:, columns] = up
                down_sum[columns] = piece[2].astype(F32).T
                terms = gate * gate_w[:, columns].astype(F32) + up * up_w[:, columns].astype(F32)
                for spot in range(0, terms.shape[1], HD):
                    total += terms[:, spot : spot + HD]
            gain[...] = total


def feed_sums(place, sums, others, w_gate, w_up):
    rows = others[0].shape[1]
    hidden = w_gate.shape[1]

    def half(step, place):
        return place[0] ^ step

    weight = pl.BlockSpec((rows, hidden // 2), lambda step, place: (place[3], half(step, place)))
    wide = pl.BlockSpec((rows, hidden // 2), lambda step, place: (0, half(step, place)))
    tall = pl.BlockSpec((hidden // 2, rows), lambda step, place: (half(step, place), 0))
    return call(
        functools.partial(feed_sums_kernel, len(sums)),
        place,
        (2,),
        [whole(piece.shape) for piece in (*sums, *others)] + [weight] * 2,
        [wide, wide, tall, whole((rows, HD))],
        [
            array((rows, hidden), F32),
            array((rows, hidden), F32),
            array((hidden, rows), F32),
            array((rows, HD), F32),
        ],
        [],
        moved=45 * rows * hidden,
    )(place, *sums, *others, w_gate, w_up)


def local(
    activations,
    doc_ids,
    w_query,
    w_key,
    w_value,
    w_out,
    w_gate,
    w_up,
    w_down,
    gain_attn,
    gain_mlp,
    cotangent,
):
    rows, width = activations.shape
    devices = lax.axis_size("seq")
    total = rows * devices
    features = width // devices
    local_width = w_query.shape[1]
    heads = local_width // HD
    share = devices // (2 * heads)
    me = lax.axis_index("seq")
    core = me % 2
    residue = (me // 2) % share
    head = me // (2 * share)
    tiles = w_gate.shape[1] // 2 // TILE
    feed_weights = (w_gate, w_up, w_down)

    def place(a, r, c):
        return (a * share + r) * 2 + c

    def split(s):
        return s // (2 * share), (s // 2) % share, s % 2

    def permuted(x, target):
        return lax.ppermute(x, "seq", [(s, target(*split(s))) for s in range(devices)])

    def core_swap(x):
        return permuted(x, lambda a, r, c: place(a, r, 1 - c))

    def pair_swap(x):
        return permuted(x, lambda a, r, c: place(a ^ 1, r, c))

    ring = (*range(0, heads, 2), *range(heads - 1, 0, -2))
    spots = [ring.index(a) for a in range(heads)]
    ring_groups = [[place(a, r, c) for a in ring] for r in range(share) for c in range(2)]

    def gathered(x):
        return lax.all_gather(x, "seq", axis=0, tiled=True, axis_index_groups=ring_groups)

    def head_swap(x):
        return lax.ppermute(x, "head", [(0, 1), (1, 0)])

    share_groups = [
        [place(a, r, c) for r in range(share)] for a in range(heads) for c in range(2)
    ]

    def after(x, *earlier):
        return lax.optimization_barrier((x, *earlier))[0]

    def exchange(x):
        return lax.all_to_all(x, "seq", 0, 0, tiled=True, axis_index_groups=ring_groups)

    def by_head(x):
        return jnp.stack([x[spot] for spot in spots])

    def share_sum(x, dim):
        if share == 1:
            return x
        return lax.psum_scatter(
            x, "seq", scatter_dimension=dim, tiled=True, axis_index_groups=share_groups
        )

    def in_core_order(mine, other, axis):
        return jnp.where(core == 0, jnp.stack([mine, other], axis), jnp.stack([other, mine], axis))

    def my_part(x, index, axis):
        return lax.dynamic_index_in_dim(x, index, axis, keepdims=False)

    column = lax.axis_index("head")

    def my_half(x):
        return lax.dynamic_slice_in_dim(x, column * (width // 2), width // 2, 1)

    last = []

    def following(x):
        return after(x, *last)

    def done(x):
        last[:] = [x]
        return x

    my_places = me * rows + jnp.arange(rows, dtype=jnp.int32)
    block_starts = place(jnp.array(ring, jnp.int32), residue, core) * rows
    query_places = block_starts[:, None] + jnp.arange(rows, dtype=jnp.int32)[None, :]
    query_docs = doc_ids.reshape(heads, share, 2, rows)[jnp.array(ring), residue, core]
    query_starts = jnp.sum((doc_ids < query_docs[..., None]).astype(jnp.int32), -1)
    key_places = jnp.arange(total, dtype=jnp.int32)
    allowed = (key_places >= query_starts.reshape(-1, 1)) & (
        key_places <= query_places.reshape(-1, 1)
    )
    scale = HD ** (-0.5)
    core_index = core[None].astype(jnp.int32)
    spot_index = jnp.array(spots, jnp.int32)
    position = jnp.concatenate([jnp.stack([head % 2, head // 2, core, me, column]), spot_index]).astype(jnp.int32)

    plane_cotangent = gathered(cotangent)
    inputs = activations.astype(F32)
    cosine, sine = turning(my_places, 1.0)
    normed_low, blocks = head_blocks(
        spot_index, activations, gain_attn, cosine, sine, w_query, w_key, w_value
    )
    chip_cotangent = jnp.concatenate([cotangent, core_swap(cotangent)], 0)
    early_tiles = tiles * 4 // 8
    late_tiles = tiles - early_tiles
    def hidden_grads(grads, half, first, count):
        start = (half * tiles + first) * TILE
        return dot_back(grads, lax.dynamic_slice_in_dim(w_down, start, count * TILE, 0)).astype(BF16)

    chip_grads = after(chip_cotangent, blocks)
    chip_hidden_grad = hidden_grads(chip_grads, core, 0, tiles)
    head_rows = after(exchange(blocks), chip_hidden_grad, query_starts)

    def all_keys(own):
        if share > 1:
            own = lax.all_gather(own, "seq", axis=1, axis_index_groups=share_groups)
        else:
            own = own[:, None]
        return in_core_order(own, core_swap(own), 2).reshape(total, 2 * HD)

    head_kv = all_keys(by_head(head_rows[:, :, HD:]))
    scores = dot_back(head_rows[:, :, :HD].reshape(heads * rows, HD), head_kv[:, :HD])
    weights = jnp.where(allowed, jax.nn.sigmoid(scores * scale - math.log(BIAS_LEN)), 0.0)
    head_mixed = dot(weights.astype(BF16), head_kv[:, HD:]).astype(BF16)
    attended = by_head(exchange(head_mixed.reshape(heads, rows, HD)))
    attended = attended.transpose(1, 0, 2).reshape(rows, -1)

    branch = dot(attended, w_out).astype(BF16)
    branch_received = head_swap(branch)
    cosines, sines = turning(after(query_places, branch), -1.0)
    first_hidden_grad = hidden_grads(
        after(plane_cotangent, branch, cosines, sines), head % 2, 0, early_tiles
    )
    branch_received = after(branch_received, first_hidden_grad)
    middle = inputs + (branch.astype(F32) + branch_received.astype(F32))
    second, _ = normalized(middle, gain_mlp)
    second_low = second.astype(BF16)
    plane_second = gathered(second_low)

    back_own, back_other, hidden = chip_back(
        core_index, second_low, core_swap(second_low), chip_hidden_grad, feed_weights
    )

    def core_sum(own, other):
        return (own + core_swap(other).astype(F32)).astype(BF16)

    back_low = core_sum(back_own, back_other)
    back_received = head_swap(back_low)
    done(back_low)
    last_hidden_grad = done(hidden_grads(following(plane_cotangent), head % 2, early_tiles, late_tiles))
    feed_own, feed_other = chip_feed(core_index, following(hidden), w_down)
    done(feed_own)
    upstream = back_low.astype(F32) + following(back_received).astype(F32)
    inverse = lax.rsqrt(jnp.mean(middle * middle, axis=-1, keepdims=True) + 1e-05)
    middle_grad = cotangent.astype(F32) + norm_back(middle, inverse, gain_mlp, upstream)
    branch_low = middle_grad.astype(BF16)
    blocks = joined(spot_index, heads, dot_back(branch_low, w_out).astype(BF16), branch_low)
    done(blocks)
    own_normed = gathered(following(my_half(normed_low)))
    upstream = exchange(blocks)
    feed_low = done(core_sum(following(feed_own), feed_other))
    feed_received = head_swap(feed_low)

    def plane_piece(first, count, hidden_grad):
        kept, given = plane_weight_grads(
            position,
            share,
            following(plane_second),
            plane_cotangent,
            hidden_grad,
            feed_weights,
            first,
            count,
        )
        done(given)
        return kept, core_swap(given)

    def plane_halves(kept, received):
        def half(pair):
            parts = [x.reshape(3, 2, share * features, -1) for x in (following(kept), received)]
            part = sum(my_part(x, pair, 1).astype(F32) for x in parts)
            part = share_sum(part.reshape(3, share, features, -1), 1).reshape(3, features, -1)
            return done(part.astype(BF16))

        other = pair_swap(half(1 - head % 2))
        return half(head % 2), other

    first_piece = plane_piece(0, early_tiles, first_hidden_grad)
    feed = following(feed_low).astype(F32) + feed_received.astype(F32)
    output = done((middle + feed).astype(BF16))
    upstream = following(upstream)
    query_grad, own_grad, other_grad = attention_back(
        position,
        share,
        ring,
        head_rows,
        head_kv,
        upstream,
        query_starts,
        query_places,
        cosines,
        sines,
    )
    done(other_grad)
    all_attended = gathered(following(attended))
    received = core_swap(other_grad)
    if share > 1:
        shape = (heads, share, rows, 2 * HD)
        own_grad = share_sum((own_grad + received.astype(F32)).reshape(shape), 1)[:, 0]
        received = jnp.zeros(own_grad.shape, BF16)
    ring_grads = done(
        grad_blocks(position, ring, following(query_grad), own_grad, received, cosines, sines)
    )
    received = exchange(ring_grads)
    other_normed = head_swap(after(own_normed, ring_grads))
    first_halves = plane_halves(*first_piece)
    last_piece = plane_piece(early_tiles, late_tiles, last_hidden_grad)

    normed_part = done(projected_back(position, ring, following(received), w_query, w_key, w_value))
    normed_received = head_swap(normed_part)
    last_halves = plane_halves(*last_piece)
    own_sum, other_sum = attention_weight_grads(
        position,
        share,
        heads,
        own_normed,
        other_normed,
        following(ring_grads).reshape(heads * rows, -1),
    )
    done(other_sum)
    other_received = core_swap(other_sum)
    if share > 1:
        own_sum = own_sum.astype(F32) + other_received.astype(F32)
        own_sum = own_sum.reshape(heads, share, features, -1)
        own_sum = share_sum(own_sum, 1)[:, 0]
        other_received = jnp.zeros(own_sum.shape, BF16)
    own_sum = after(own_sum, last_halves[1])
    sum_received = exchange(done((following(own_sum).astype(F32) + other_received.astype(F32)).astype(BF16)))
    out_part = done(dot_rows(following(all_attended), following(upstream)[:, :, HD:].reshape(heads * rows, -1)))
    out_part = out_part.reshape(local_width, share, 2, features)
    out_given = done(my_part(out_part, 1 - core, 2).astype(BF16))
    out_sum = my_part(out_part, core, 2) + core_swap(out_given).astype(F32)
    out_sum = share_sum(out_sum, 1).reshape(local_width, features)
    normed_grad = following(normed_part).astype(F32) + normed_received.astype(F32)
    inverse_attn = lax.rsqrt(jnp.mean(inputs * inputs, axis=-1, keepdims=True) + 1e-05)
    input_grad = (middle_grad + norm_back(inputs, inverse_attn, gain_attn, normed_grad)).astype(BF16)
    done(input_grad)

    gate_sum, up_sum, down_sum, feed_gain = feed_sums(
        position,
        [following(first_halves[0]), last_halves[0]],
        [first_halves[1], last_halves[1]],
        w_gate,
        w_up,
    )
    done(feed_gain)
    query_sum, key_sum, value_sum, attention_gain = attention_sums(
        position,
        ring,
        following(sum_received),
        (w_query, w_key, w_value),
    )

    def gain_sum(terms, gain):
        return jnp.sum(terms, axis=1) / lax.dynamic_slice_in_dim(gain, me * features, features, 0)

    gains = jnp.stack([gain_sum(attention_gain.T, gain_attn), gain_sum(feed_gain, gain_mlp)])
    gains = gains + head_swap(gains)
    return (
        output,
        input_grad,
        query_sum,
        key_sum,
        value_sum,
        out_sum,
        gate_sum,
        up_sum,
        down_sum,
        gains[0],
        gains[1],
    )


def solution(mesh):
    placed = (
        P("seq", None),
        P(),
        P(None, "head"),
        P(None, "head"),
        P(None, "head"),
        P("head", None),
        P(None, "head"),
        P(None, "head"),
        P("head", None),
        P(),
        P(),
        P("seq", None),
    )
    return jax.shard_map(
        local,
        mesh=mesh,
        in_specs=placed,
        out_specs=(
            P("seq", None),
            P("seq", None),
            P("seq", "head"),
            P("seq", "head"),
            P("seq", "head"),
            P("head", "seq"),
            P("seq", "head"),
            P("seq", "head"),
            P("head", "seq"),
            P("seq"),
            P("seq"),
        ),
        check_vma=False,
    )
```
